32 devices in a mesh: group: 16 (over z, y, x), kv: 2 (over core).
Axes of the slice: x: 2, y: 2, z: 4, core: 2. Of those that a mesh axis runs over, the one named last changes fastest.
Arguments:
- lengths: int32 [16], P('group'), may hold values from 2048 to 8192, as said below
- latents: bfloat16 [16, 8192, 160], P('group', 'kv'), may hold values from -6 to 6
- codes: bfloat16 [16, 8192, 1024], P('group', 'kv'), may hold values from -10 to 10
- scales: bfloat16 [16, 32, 8], P('group', 'kv'), may hold values from 0.5 to 4
- queries: bfloat16 [16, 8, 8192], P('group'), may hold values from -900 to 900
- new_keys: bfloat16 [16, 8, 1024], P('group'), may hold values from -8 to 8
- new_values: bfloat16 [16, 8, 1024], P('group'), may hold values from -12 to 12
- key_factor: bfloat16 [160, 1024], replicated, may hold values from -0.5 to 0.5
- out_weight: bfloat16 [8192, 8192], P('kv', 'group'), may hold values from -0.0625 to 0.0625
Outputs:
- layer_out: float32 [128, 8192], P('kv', 'group')
The draws below stay inside these ranges and needn't reach their ends.
Inputs may be any that keep to these rules, and one draw needn't show every extreme that they name: `lengths`: one request has exactly 8192 cached tokens and one exactly 2048.
All inputs are finite; a program needn't handle non-finite values.
Results may differ from the reference program's by a relative error of at most 0.0087.
Values may be sent and summed in bfloat16 or wider, within the bound.
A program may use at most 128 MiB of HBM per device.

```python
import math
import jax
import jax.numpy as jnp
from jax import lax

D = 8192
HEADS = 64
KV_HEADS = 8
HEAD_DIM = 128
RANK = 160
BLK = 256
Q_TOK = 8
REQS = 16
CTX = 8192


def drawn_base(key):
    return jax.random.normal(key, (REQS, Q_TOK, KV_HEADS, 1, HEAD_DIM), jnp.float32)


def draw_lengths(key, part):
    key = jax.random.fold_in(key, 11)
    key_tier, key_fill, key_top, key_low = jax.random.split(key, 4)
    tier_pick = jax.random.randint(key_tier, (REQS,), 0, 3)
    lowest = jnp.where(tier_pick == 2, CTX // 2, CTX // 4)
    spread = jnp.where(tier_pick == 2, CTX - CTX // 2, CTX // 2 - CTX // 4)
    drawn = lowest + jax.random.randint(key_fill, (REQS,), 0, 1 << 24) % spread
    top_index = jax.random.randint(key_top, (), 0, REQS)
    low_index = (top_index + 1 + jax.random.randint(key_low, (), 0, REQS - 1)) % REQS
    drawn = drawn.at[top_index].set(CTX).at[low_index].set(CTX // 4)
    return drawn.astype(jnp.int32)


def draw_codes(key, part):
    key = jax.random.fold_in(key, 23)
    key_centre, key_noise = jax.random.split(key)
    centre = jax.random.normal(key_centre, (REQS, 1, KV_HEADS * HEAD_DIM), jnp.float32)
    noise = jax.random.normal(key_noise, (REQS, CTX, KV_HEADS * HEAD_DIM), jnp.float32)
    return jnp.clip(centre + noise, -10.0, 10.0).astype(jnp.bfloat16)


def draw_queries(key, part):
    common = drawn_base(key)
    key = jax.random.fold_in(key, 31)
    key_noise = jax.random.fold_in(key, 0)
    noise = jax.random.normal(key_noise, (REQS, Q_TOK, KV_HEADS, HEADS // KV_HEADS, HEAD_DIM), jnp.float32)
    drawn = 1.05 * (common + noise)
    return jnp.clip(drawn, -900.0, 900.0).reshape(REQS, Q_TOK, HEADS * HEAD_DIM).astype(jnp.bfloat16)


def draw_new_keys(key, part):
    common = drawn_base(key)[:, :, :, 0, :]
    key = jax.random.fold_in(key, 37)
    noise = jax.random.normal(key, (REQS, Q_TOK, KV_HEADS, HEAD_DIM), jnp.float32)
    drawn = 0.7 * common + 0.3 * noise
    return jnp.clip(drawn, -8.0, 8.0).reshape(REQS, Q_TOK, KV_HEADS * HEAD_DIM).astype(jnp.bfloat16)


def block_levels(stream_key, dims, cuts, least, largest):
    gain, own = 1.0, jax.random.fold_in(stream_key, 6)
    for axis_at, parts in cuts:
        draws = jnp.exp(jax.random.uniform(jax.random.fold_in(own, axis_at), (parts,), jnp.float32, least / len(cuts), largest / len(cuts)))
        gain = gain * jnp.repeat(draws, dims[axis_at] // parts).reshape([-1 if axis == axis_at else 1 for axis in range(len(dims))])
    return gain


def normal_values(own_key, extent, deviation, bound, shards=(), kind=jnp.bfloat16):
    values = deviation * jax.random.normal(own_key, extent, jnp.float32)
    if shards:
        values = values * block_levels(own_key, extent, shards, -0.22, 0.18)
    return jnp.clip(values, -bound, bound).astype(kind)


def setup_inputs(seed: int = 0) -> dict:
    keys = jax.random.split(jax.random.key(seed), 10)
    lengths = draw_lengths(jax.random.fold_in(keys[9], 71), 0)
    latents = normal_values(keys[1], (REQS, CTX, RANK), 1.0, 6.0, ((0, 16), (1, 2)))
    codes = draw_codes(jax.random.fold_in(keys[9], 71), 0)
    scales = jnp.clip(jnp.exp(math.log(4.0) - 2.0794415 * jax.random.uniform(keys[3], (REQS, CTX // BLK, KV_HEADS), jnp.float32) ** block_levels(keys[3], (REQS, CTX // BLK, KV_HEADS), ((0, 16), (1, 2)), -0.2, 0.2)), 0.5, 4.0).astype(jnp.bfloat16)
    queries = draw_queries(jax.random.fold_in(keys[9], 71), 0)
    new_keys = draw_new_keys(jax.random.fold_in(keys[9], 71), 0)
    new_values = normal_values(keys[6], (REQS, Q_TOK, KV_HEADS * HEAD_DIM), 2.0, 12.0, ((0, 16),))
    key_factor = normal_values(keys[7], (RANK, KV_HEADS * HEAD_DIM), RANK ** -0.5, 0.5)
    out_weight = normal_values(keys[8], (HEADS * HEAD_DIM, D), (HEADS * HEAD_DIM) ** -0.5, 0.0625, ((0, 2), (1, 16)))
    return dict(lengths=lengths, latents=latents, codes=codes, scales=scales, queries=queries, new_keys=new_keys, new_values=new_values, key_factor=key_factor, out_weight=out_weight)


ROPE_BASE = 500000.0
NEG_FILL = -1.0e30


def rotate(key_before_rotary, positions):
    half_dim = HEAD_DIM // 2
    frequency = ROPE_BASE ** (-(jnp.arange(half_dim, dtype=jnp.float32) * 2.0) / HEAD_DIM)
    angles = positions.astype(jnp.float32)[:, None] * frequency[None, :]
    cosine = jnp.cos(angles)[:, None, :]
    sine_val = jnp.sin(angles)[:, None, :]
    lower_half = key_before_rotary[..., :half_dim]
    upper_half = key_before_rotary[..., half_dim:]
    return jnp.concatenate([lower_half * cosine - upper_half * sine_val, upper_half * cosine + lower_half * sine_val], axis=-1)


def reference(lengths, latents, codes, scales, queries, new_keys, new_values, key_factor, out_weight):
    groups = HEADS // KV_HEADS
    score_scale = HEAD_DIM ** -0.5

    def single_request(request_item):
        latent, code_rows, scale_rows, query_matrix_rows, fresh_keys, fresh_values, length = request_item
        key_before_rotary = jnp.dot(latent, key_factor, preferred_element_type=jnp.float32).reshape(CTX, KV_HEADS, HEAD_DIM)
        rotary_applied = rotate(key_before_rotary, jnp.arange(CTX, dtype=jnp.int32)).astype(jnp.bfloat16)
        rotary_applied = lax.optimization_barrier(rotary_applied).astype(jnp.float32)
        query_f = query_matrix_rows.astype(jnp.float32).reshape(Q_TOK, KV_HEADS, groups, HEAD_DIM)
        cache_scores = jnp.einsum('tkgd,ckd->tkgc', query_f, rotary_applied) * score_scale
        valid_mask = (jnp.arange(CTX, dtype=jnp.int32) < length)[None, None, None, :]
        cache_scores = jnp.where(valid_mask, cache_scores, NEG_FILL)
        fresh_f = fresh_keys.astype(jnp.float32).reshape(Q_TOK, KV_HEADS, HEAD_DIM)
        fresh_scores = jnp.einsum('tkgd,ukd->tkgu', query_f, fresh_f) * score_scale
        order_mask = jnp.arange(Q_TOK)[None, :] <= jnp.arange(Q_TOK)[:, None]
        causal = order_mask[:, None, None, :]
        fresh_scores = jnp.where(causal, fresh_scores, NEG_FILL)
        peak_score = jnp.maximum(jnp.max(cache_scores, axis=-1), jnp.max(fresh_scores, axis=-1))
        cache_weights = jnp.where(valid_mask, jnp.exp(cache_scores - peak_score[..., None]), 0.0)
        fresh_weights = jnp.where(causal, jnp.exp(fresh_scores - peak_score[..., None]), 0.0)
        totals = jnp.sum(cache_weights, axis=-1) + jnp.sum(fresh_weights, axis=-1)
        cache_rounded = lax.optimization_barrier(cache_weights.astype(jnp.bfloat16)).astype(jnp.float32)
        fresh_rounded = lax.optimization_barrier(fresh_weights.astype(jnp.bfloat16)).astype(jnp.float32)
        values = code_rows.astype(jnp.float32).reshape(CTX // BLK, BLK, KV_HEADS, HEAD_DIM)
        values = (values * scale_rows.astype(jnp.float32)[:, None, :, None]).reshape(CTX, KV_HEADS, HEAD_DIM)
        fresh_vals = fresh_values.astype(jnp.float32).reshape(Q_TOK, KV_HEADS, HEAD_DIM)
        numerator = jnp.einsum('tkgc,ckd->tkgd', cache_rounded, values) + jnp.einsum('tkgu,ukd->tkgd', fresh_rounded, fresh_vals)
        attended = numerator / totals[..., None]
        return attended.reshape(Q_TOK, HEADS * HEAD_DIM).astype(jnp.bfloat16)

    attended_all = lax.map(single_request, (latents, codes, scales, queries, new_keys, new_values, lengths))
    all_rows = attended_all.reshape(REQS * Q_TOK, HEADS * HEAD_DIM)
    return jnp.dot(all_rows, out_weight, preferred_element_type=jnp.float32)
```

```python
import functools
import math

import jax
import jax.numpy as jnp
import numpy as np
from jax import lax
from jax.experimental import pallas as pl
from jax.experimental.pallas import tpu as pltpu
from jax.sharding import PartitionSpec as P

HEADS = 64
KV_HEADS = 8
GROUPS = HEADS // KV_HEADS
HEAD_DIM = 128
HALF = HEAD_DIM // 2
BLK = 256
Q_TOK = 8
ROWS = Q_TOK * GROUPS
PAIR = 2
CHUNK = 512
ROPE_BASE = 500000.0
NEG_FILL = -1e30
TO_EXP2 = math.log2(math.e) / math.sqrt(HEAD_DIM)
MESH = pl.DeviceIdType.MESH
F32 = jnp.float32
BF16 = jnp.bfloat16


def rope_tables(ctx):
    exponent = -(np.arange(HALF, dtype=np.float64) * 2.0) / HEAD_DIM
    frequency = (ROPE_BASE**exponent).astype(np.float32)
    angles = frequency[:, None] * np.arange(ctx, dtype=np.float32)[None, :]
    angles = angles.astype(np.float64)
    return np.cos(angles).astype(np.float32), np.sin(angles).astype(np.float32)


def stacked_rows(block):
    wide = block.astype(F32)
    return jnp.concatenate(
        [wide[:, g * HEAD_DIM : (g + 1) * HEAD_DIM] for g in range(GROUPS)], axis=0
    ).astype(BF16)


def padded(block):
    wide = block.astype(F32)
    blank = jnp.zeros((HEAD_DIM - Q_TOK, HEAD_DIM), F32)
    return jnp.concatenate([wide, blank], axis=0).astype(BF16)


def attend_kernel(
    place, scales, latents, factor, cosine, sine, queries, codes, new_keys, new_values,
    numer, stats, scores,
):
    pair = pl.program_id(0)
    at, length = place[0], place[1]
    own = latents.shape[0]
    base = at * own
    turned = factor[...].astype(F32).T.astype(BF16)
    query = [
        stacked_rows(queries[:, i * GROUPS * HEAD_DIM : (i + 1) * GROUPS * HEAD_DIM])
        for i in range(PAIR)
    ]
    tops = [jnp.full((ROWS, HEAD_DIM), NEG_FILL, F32) for _ in range(PAIR)]
    for c in range(own // CHUNK):
        span = slice(c * CHUNK, (c + 1) * CHUNK)
        keys = lax.dot_general(
            turned, latents[span, :], (((1,), (1,)), ((), ())), preferred_element_type=F32
        )
        cos, sin = cosine[:, span], sine[:, span]
        position = base + c * CHUNK + lax.broadcasted_iota(jnp.int32, (1, CHUNK), 1)
        valid = position < length
        for i in range(PAIR):
            low = keys[i * HEAD_DIM : i * HEAD_DIM + HALF]
            high = keys[i * HEAD_DIM + HALF : (i + 1) * HEAD_DIM]
            rotated = jnp.concatenate(
                [low * cos - high * sin, high * cos + low * sin], axis=0
            ).astype(BF16)
            score = jnp.dot(query[i], rotated, preferred_element_type=F32)
            score = jnp.where(valid, score, NEG_FILL)
            scores[i, :, span] = score
            for v in range(CHUNK // HEAD_DIM):
                tops[i] = jnp.maximum(tops[i], score[:, v * HEAD_DIM : (v + 1) * HEAD_DIM])
    column = lax.broadcasted_iota(jnp.int32, (ROWS, HEAD_DIM), 1)
    token = lax.broadcasted_iota(jnp.int32, (ROWS, HEAD_DIM), 0) % Q_TOK
    causal = jnp.logical_and(column <= token, at == 0)
    for i in range(PAIR):
        lanes = slice(i * HEAD_DIM, (i + 1) * HEAD_DIM)
        fresh = lax.dot_general(
            query[i], padded(new_keys[:, lanes]), (((1,), (1,)), ((), ())),
            preferred_element_type=F32,
        )
        fresh = jnp.where(causal, fresh, NEG_FILL)
        peak = jnp.max(jnp.maximum(tops[i], fresh), axis=1, keepdims=True) * TO_EXP2
        weight = jnp.where(causal, jnp.exp2(fresh * TO_EXP2 - peak), 0.0)
        total = weight
        part = jnp.dot(weight.astype(BF16), padded(new_values[:, lanes]), preferred_element_type=F32)
        for b in range(own // BLK):
            span = slice(b * BLK, (b + 1) * BLK)
            weight = jnp.exp2(scores[i, :, span] * TO_EXP2 - peak)
            for v in range(BLK // HEAD_DIM):
                total = total + weight[:, v * HEAD_DIM : (v + 1) * HEAD_DIM]
            product = jnp.dot(weight.astype(BF16), codes[span, lanes], preferred_element_type=F32)
            part = part + product * scales[b, pair * PAIR + i]
        total = jnp.sum(total, axis=1, keepdims=True)
        numer[i] = part
        stats[i] = jnp.where(column < HALF, peak, total)


def attend(place, scales, latents, factor, queries, codes, new_keys, new_values, ctx):
    own, rank = latents.shape
    cosine, sine = rope_tables(ctx)
    wide = PAIR * HEAD_DIM
    vmem = lambda shape, index: pl.BlockSpec(shape, index)
    shape = jax.ShapeDtypeStruct((KV_HEADS, ROWS, HEAD_DIM), F32)
    return pl.pallas_call(
        attend_kernel,
        out_shape=(shape, shape),
        grid_spec=pltpu.PrefetchScalarGridSpec(
            num_scalar_prefetch=2,
            grid=(KV_HEADS // PAIR,),
            in_specs=[
                vmem((own, rank), lambda j, p, s: (0, 0)),
                vmem((rank, wide), lambda j, p, s: (0, j)),
                vmem((HALF, own), lambda j, p, s: (0, p[0])),
                vmem((HALF, own), lambda j, p, s: (0, p[0])),
                vmem((Q_TOK, GROUPS * wide), lambda j, p, s: (0, j)),
                vmem((own, wide), lambda j, p, s: (0, j)),
                vmem((Q_TOK, wide), lambda j, p, s: (0, j)),
                vmem((Q_TOK, wide), lambda j, p, s: (0, j)),
            ],
            out_specs=[
                vmem((PAIR, ROWS, HEAD_DIM), lambda j, p, s: (j, 0, 0)),
                vmem((PAIR, ROWS, HEAD_DIM), lambda j, p, s: (j, 0, 0)),
            ],
            scratch_shapes=[pltpu.VMEM((PAIR, ROWS, own), F32)],
        ),
        compiler_params=pltpu.CompilerParams(vmem_limit_bytes=48 * 1024 * 1024),
        name="attend",
    )(place, scales, latents, factor, jnp.asarray(cosine), jnp.asarray(sine), queries, codes,
      new_keys, new_values)


def lattice(size):
    return {16: (4, 2, 2), 64: (4, 4, 4)}.get(size, (size, 1, 1))


def gather_chain(buffer, order, axis, sizes, spot, group_of, send, recv):
    size, mine = sizes[axis], spot[axis]

    def block(index):
        where = []
        for a in range(3):
            if a == axis:
                where.append(index)
            elif a in order:
                where.append(slice(None))
            else:
                where.append(spot[a])
        return buffer.at[tuple(where)]

    def neighbour(step):
        there = list(spot)
        there[axis] = there[axis] + step
        return group_of(there)

    def copy(index, direction, step):
        to = neighbour(1 if direction == 0 else -1)
        return pltpu.make_async_remote_copy(
            src_ref=block(index),
            dst_ref=block(index),
            send_sem=send.at[axis, direction, step],
            recv_sem=recv.at[axis, direction, step],
            device_id=(to, lax.axis_index("kv")),
            device_id_type=MESH,
        )

    up = lambda s: jnp.logical_and(mine - s >= 0, mine < size - 1)
    down = lambda s: jnp.logical_and(mine + s < size, mine > 0)

    def begin(s):
        @pl.when(up(s))
        def _():
            copy(mine - s, 0, s).start()

        @pl.when(down(s))
        def _():
            copy(mine + s, 1, s).start()

    def arrive(s):
        @pl.when(mine - 1 - s >= 0)
        def _():
            copy(mine - 1 - s, 0, s).wait_recv()

        @pl.when(mine + 1 + s < size)
        def _():
            copy(mine + 1 + s, 1, s).wait_recv()

    def finish(s):
        @pl.when(up(s))
        def _():
            copy(mine - s, 0, s).wait_send()

        @pl.when(down(s))
        def _():
            copy(mine + s, 1, s).wait_send()

    return size - 1, begin, arrive, finish


def project_kernel(
    sizes, numer, stats, weight_hbm, out,
    weight, got_numer, got_stats, buffer, rows, partial, got_partial,
    weight_sem, pair_send, pair_recv, send, recv,
):
    at = lax.axis_index("kv")
    other = 1 - at
    me = lax.axis_index("group")
    z_size, y_size, x_size = sizes
    spot = [me // (y_size * x_size), me // x_size % y_size, me % x_size]
    group_of = lambda s: (s[0] * y_size + s[1]) * x_size + s[2]

    barrier = pltpu.get_barrier_semaphore()
    pl.semaphore_signal(barrier, inc=1, device_id=(me, other), device_id_type=MESH)
    expected = 1
    for axis in range(3):
        for step in (-1, 1):
            if sizes[axis] == 1:
                continue
            inside = jnp.logical_and(spot[axis] + step >= 0, spot[axis] + step < sizes[axis])
            there = list(spot)
            there[axis] = there[axis] + step

            @pl.when(inside)
            def _(there=there):
                pl.semaphore_signal(
                    barrier, inc=1, device_id=(group_of(there), at), device_id_type=MESH
                )

            expected = expected + inside.astype(jnp.int32)
    load = pltpu.make_async_copy(weight_hbm, weight, weight_sem)
    load.start()
    pl.semaphore_wait(barrier, expected)

    half_heads = KV_HEADS // 2
    pair_copy = lambda n, src, dst: pltpu.make_async_remote_copy(
        src_ref=src, dst_ref=dst, send_sem=pair_send.at[n], recv_sem=pair_recv.at[n],
        device_id=(me, other), device_id_type=MESH,
    )
    theirs = pl.ds(other * half_heads, half_heads)
    first = pair_copy(0, stats.at[theirs], got_stats)
    second = pair_copy(1, numer.at[theirs], got_numer)
    first.start()
    second.start()
    first.wait()
    second.wait()
    for k in range(half_heads):
        mine_stat, their_stat = stats[at * half_heads + k], got_stats[k]
        mine_peak, mine_total = mine_stat[:, :1], mine_stat[:, HALF : HALF + 1]
        their_peak, their_total = their_stat[:, :1], their_stat[:, HALF : HALF + 1]
        peak = jnp.maximum(mine_peak, their_peak)
        mine_scale, their_scale = jnp.exp2(mine_peak - peak), jnp.exp2(their_peak - peak)
        total = mine_total * mine_scale + their_total * their_scale
        joined = numer[at * half_heads + k] * mine_scale + got_numer[k] * their_scale
        buffer[k // 2, spot[0], spot[1], spot[2], (k % 2) * ROWS : (k % 2 + 1) * ROWS] = (
            joined / total
        ).astype(BF16)

    orders = ((0, 1, 2), (0, 2, 1))
    for stage in range(3):
        chains = [
            gather_chain(
                buffer.at[c], orders[c][:stage], orders[c][stage], sizes, spot, group_of,
                send.at[c], recv.at[c],
            )
            for c in range(2)
        ]
        for s in range(max(chain[0] for chain in chains)):
            for steps, begin, arrive, finish in chains:
                if s < steps:
                    begin(s)
            for steps, begin, arrive, finish in chains:
                if s < steps:
                    arrive(s)
        for steps, begin, arrive, finish in chains:
            for s in range(steps):
                finish(s)

    members = z_size * y_size * x_size
    for k in range(half_heads):
        block = buffer[k // 2, :, :, :, (k % 2) * ROWS : (k % 2 + 1) * ROWS, :]
        block = block.reshape(members, ROWS, HEAD_DIM).astype(F32)
        for g in range(GROUPS):
            piece = block[:, g * Q_TOK : (g + 1) * Q_TOK, :]
            feature = (k * GROUPS + g) * HEAD_DIM
            rows[:, feature : feature + HEAD_DIM] = piece.reshape(
                members * Q_TOK, HEAD_DIM
            ).astype(BF16)
    load.wait()
    partial[...] = jnp.dot(rows[...], weight[...], preferred_element_type=F32)
    half_rows = members * Q_TOK // 2
    last = pair_copy(2, partial.at[pl.ds(other * half_rows, half_rows)], got_partial)
    last.start()
    last.wait()
    out[...] = partial[pl.ds(at * half_rows, half_rows)] + got_partial[...]


def project(numer, stats, out_weight, members):
    depth, columns = out_weight.shape
    sizes = lattice(members)
    half = KV_HEADS // 2
    count = members * Q_TOK
    longest = max(max(sizes) - 1, 1)
    return pl.pallas_call(
        functools.partial(project_kernel, sizes),
        out_shape=jax.ShapeDtypeStruct((count // 2, columns), F32),
        in_specs=[
            pl.BlockSpec(memory_space=pltpu.VMEM),
            pl.BlockSpec(memory_space=pltpu.VMEM),
            pl.BlockSpec(memory_space=pl.ANY),
        ],
        out_specs=pl.BlockSpec(memory_space=pltpu.VMEM),
        scratch_shapes=[
            pltpu.VMEM((depth, columns), BF16),
            pltpu.VMEM((half, ROWS, HEAD_DIM), F32),
            pltpu.VMEM((half, ROWS, HEAD_DIM), F32),
            pltpu.VMEM((2, *sizes, half // 2 * ROWS, HEAD_DIM), BF16),
            pltpu.VMEM((count, depth), BF16),
            pltpu.VMEM((count, columns), F32),
            pltpu.VMEM((count // 2, columns), F32),
            pltpu.SemaphoreType.DMA,
            pltpu.SemaphoreType.DMA((3,)),
            pltpu.SemaphoreType.DMA((3,)),
            pltpu.SemaphoreType.DMA((2, 3, 2, longest)),
            pltpu.SemaphoreType.DMA((2, 3, 2, longest)),
        ],
        compiler_params=pltpu.CompilerParams(
            collective_id=0, has_side_effects=True, vmem_limit_bytes=48 * 1024 * 1024
        ),
        name="project",
    )(numer, stats, out_weight)


def body(lengths, latents, codes, scales, queries, new_keys, new_values, key_factor, out_weight):
    at = lax.axis_index("kv")
    ctx = latents.shape[1] * lax.axis_size("kv")
    place = jnp.stack([at.astype(jnp.int32), lengths[0]])
    numer, stats = attend(
        place, scales[0].astype(F32), latents[0], key_factor, queries[0], codes[0],
        new_keys[0], new_values[0], ctx,
    )
    return project(numer, stats, out_weight, lax.axis_size("group"))


def solution(mesh):
    placed = (
        P("group"),
        P("group", "kv", None),
        P("group", "kv", None),
        P("group", "kv", None),
        P("group", None, None),
        P("group", None, None),
        P("group", None, None),
        P(),
        P("kv", "group"),
    )
    return jax.shard_map(
        body, mesh=mesh, in_specs=placed, out_specs=P("kv", "group"), check_vma=False
    )
```

```python
import math

import jax
import jax.numpy as jnp
import numpy as np
from jax import lax
from jax.experimental import pallas as pl
from jax.experimental.pallas import tpu as pltpu
from jax.sharding import PartitionSpec as P

HEADS = 64
KV_HEADS = 8
GROUPS = HEADS // KV_HEADS
HEAD_DIM = 128
HALF = HEAD_DIM // 2
BLK = 256
Q_TOK = 8
ROWS = Q_TOK * GROUPS
PAIR = 2
CHUNK = 512
ROPE_BASE = 500000.0
NEG_FILL = -1e30
TO_EXP2 = math.log2(math.e) / math.sqrt(HEAD_DIM)
MESH = pl.DeviceIdType.MESH
F32 = jnp.float32
BF16 = jnp.bfloat16


def rope_tables(ctx):
    exponent = -(np.arange(HALF, dtype=np.float64) * 2.0) / HEAD_DIM
    frequency = (ROPE_BASE**exponent).astype(np.float32)
    angles = frequency[:, None] * np.arange(ctx, dtype=np.float32)[None, :]
    angles = angles.astype(np.float64)
    return np.cos(angles).astype(np.float32), np.sin(angles).astype(np.float32)


def stacked_rows(block):
    wide = block.astype(F32)
    return jnp.concatenate(
        [wide[:, g * HEAD_DIM : (g + 1) * HEAD_DIM] for g in range(GROUPS)], axis=0
    ).astype(BF16)


def padded(block):
    wide = block.astype(F32)
    blank = jnp.zeros((HEAD_DIM - Q_TOK, HEAD_DIM), F32)
    return jnp.concatenate([wide, blank], axis=0).astype(BF16)


def step_kernel(
    length, scales, latents_hbm, codes_hbm, cosine_hbm, sine_hbm, queries, new_keys, new_values,
    factor, weight_hbm, out,
    latents, codes, cosine, sine, weight, scores, mine, theirs, got, buffer, rows, partial,
    got_partial,
    piece_sem, codes_sem, weight_sem, pair_send, pair_recv, last_send, last_recv, send, recv,
):
    at = lax.axis_index("kv")
    other = 1 - at
    me = lax.axis_index("group")
    own = latents.shape[1]
    base = at * own
    rounds = buffer.shape[0]
    levels = buffer.ndim - 4
    members = 2**levels
    bits = [me // 2**b % 2 for b in range(levels)]
    partner = [me + (1 - 2 * bits[b]) * 2**b for b in range(levels)]
    orders = [list(range(levels))[::-1], list(range(2, levels))[::-1] + [0, 1]]
    pieces = piece_sem.shape[1]
    wide = own // pieces

    def piece_copies(n):
        span = pl.ds(n * wide, wide)
        there = pl.ds(pl.multiple_of(base + n * wide, wide), wide)
        return [
            pltpu.make_async_copy(latents_hbm.at[:, span], latents.at[:, span], piece_sem.at[0, n]),
            pltpu.make_async_copy(cosine_hbm.at[:, there], cosine.at[:, span], piece_sem.at[1, n]),
            pltpu.make_async_copy(sine_hbm.at[:, there], sine.at[:, span], piece_sem.at[2, n]),
        ]

    def head_of(r, i):
        return (at if i == 0 else other) * rounds + r

    def codes_copies(r):
        result = []
        for i in range(PAIR):
            lanes = pl.ds(pl.multiple_of(head_of(r, i) * HEAD_DIM, HEAD_DIM), HEAD_DIM)
            result.append(
                pltpu.make_async_copy(codes_hbm.at[:, lanes], codes.at[r, i], codes_sem.at[r, i])
            )
        return result

    load = pltpu.make_async_copy(weight_hbm, weight, weight_sem)
    for n in range(pieces):
        for copy in piece_copies(n):
            copy.start()
    for r in range(rounds):
        for copy in codes_copies(r):
            copy.start()
    load.start()

    barrier = pltpu.get_barrier_semaphore()
    pl.semaphore_signal(barrier, inc=1, device_id=(me, other), device_id_type=MESH)
    for b in range(levels):
        pl.semaphore_signal(barrier, inc=1, device_id=(partner[b], at), device_id_type=MESH)
    pl.semaphore_wait(barrier, levels + 1)

    def pair_copy(r):
        return pltpu.make_async_remote_copy(
            src_ref=theirs.at[r], dst_ref=got.at[r], send_sem=pair_send.at[r],
            recv_sem=pair_recv.at[r], device_id=(me, other), device_id_type=MESH,
        )

    def gather_copy(r, half, step):
        order = orders[half]
        b = order[step]
        where = [slice(None)] * levels
        for rest in order[step:]:
            where[levels - 1 - rest] = bits[rest]
        block = buffer.at[(r, half, *where)]
        return pltpu.make_async_remote_copy(
            src_ref=block, dst_ref=block, send_sem=send.at[r, half, step],
            recv_sem=recv.at[r, half, step], device_id=(partner[b], at), device_id_type=MESH,
        )

    def combine(r):
        pair_copy(r).wait()
        mine_stat, their_stat = mine[r, 1], got[r, 1]
        mine_peak, mine_total = mine_stat[:, :1], mine_stat[:, HALF : HALF + 1]
        their_peak, their_total = their_stat[:, :1], their_stat[:, HALF : HALF + 1]
        peak = jnp.maximum(mine_peak, their_peak)
        mine_scale, their_scale = jnp.exp2(mine_peak - peak), jnp.exp2(their_peak - peak)
        total = mine_total * mine_scale + their_total * their_scale
        joined = (mine[r, 0] * mine_scale + got[r, 0] * their_scale) / total
        spot = bits[::-1]
        for half in range(2):
            part = joined[half * ROWS // 2 : (half + 1) * ROWS // 2]
            buffer[(r, half, *spot)] = part.astype(BF16)
            gather_copy(r, half, 0).start()

    def relay(r, step):
        for half in range(2):
            gather_copy(r, half, step).wait()
            if step + 1 < levels:
                gather_copy(r, half, step + 1).start()

    def collect(r):
        relay(r, levels - 1)
        for half in range(2):
            block = buffer[r, half].reshape(members, ROWS // 2, HEAD_DIM).astype(F32)
            for g in range(GROUPS // 2):
                piece = block[:, g * Q_TOK : (g + 1) * Q_TOK, :]
                feature = (half * GROUPS // 2 + g) * HEAD_DIM
                rows[:, feature : feature + HEAD_DIM] = piece.reshape(
                    members * Q_TOK, HEAD_DIM
                ).astype(BF16)

    depth = GROUPS * HEAD_DIM

    def multiply(r, span):
        layer = weight[pl.ds(pl.multiple_of(r * depth, depth), depth), :]
        partial[span, :] += jnp.dot(rows[span, :], layer, preferred_element_type=F32)

    def whole_product(r):
        collect(r)

        @pl.when(r == 0)
        def _():
            load.wait()

        multiply(r, slice(None))

    column = lax.broadcasted_iota(jnp.int32, (ROWS, HEAD_DIM), 1)
    token = lax.broadcasted_iota(jnp.int32, (ROWS, HEAD_DIM), 0) % Q_TOK
    causal = jnp.logical_and(column <= token, at == 0)
    limit = length[0] - base

    def one_round(r, _):
        def hook(action):
            @pl.when(r > 0)
            def _():
                action(r - 1)

        lanes = [
            pl.ds(pl.multiple_of(head_of(r, i) * HEAD_DIM, HEAD_DIM), HEAD_DIM)
            for i in range(PAIR)
        ]
        turned = jnp.concatenate(
            [factor[:, lanes[i]].astype(F32).T for i in range(PAIR)], axis=0
        ).astype(BF16)
        query = [
            stacked_rows(queries[:, pl.ds(pl.multiple_of(head_of(r, i) * depth, depth), depth)])
            for i in range(PAIR)
        ]
        tops = [jnp.full((ROWS, HEAD_DIM), NEG_FILL, F32) for _ in range(PAIR)]
        for c in range(own // CHUNK):
            span = slice(c * CHUNK, (c + 1) * CHUNK)
            if c * CHUNK % wide == 0:

                @pl.when(r == 0)
                def _(n=c * CHUNK // wide):
                    for copy in piece_copies(n):
                        copy.wait()

            keys = jnp.dot(turned, latents[:, span], preferred_element_type=F32)
            cos, sin = cosine[:, span], sine[:, span]
            valid = c * CHUNK + lax.broadcasted_iota(jnp.int32, (1, CHUNK), 1) < limit
            for i in range(PAIR):
                low = keys[i * HEAD_DIM : i * HEAD_DIM + HALF]
                high = keys[i * HEAD_DIM + HALF : (i + 1) * HEAD_DIM]
                rotated = jnp.concatenate(
                    [low * cos - high * sin, high * cos + low * sin], axis=0
                ).astype(BF16)
                score = jnp.dot(query[i], rotated, preferred_element_type=F32)
                score = jnp.where(valid, score, NEG_FILL)
                scores[i, :, span] = score
                for v in range(CHUNK // HEAD_DIM):
                    tops[i] = jnp.maximum(tops[i], score[:, v * HEAD_DIM : (v + 1) * HEAD_DIM])
            if c == 1:
                hook(combine)
            if c >= 3 and c % 2 == 1 and (c - 3) // 2 < levels - 2:
                hook(lambda q, step=(c - 3) // 2: relay(q, step))
        for step in range(min(levels - 2, (own // CHUNK - 2) // 2), levels - 1):
            hook(lambda q, step=step: relay(q, step))
        for copy in codes_copies(r):
            copy.wait()
        for i in (1, 0):
            fresh = lax.dot_general(
                query[i], padded(new_keys[:, lanes[i]]), (((1,), (1,)), ((), ())),
                preferred_element_type=F32,
            )
            fresh = jnp.where(causal, fresh, NEG_FILL)
            peak = jnp.max(jnp.maximum(tops[i], fresh), axis=1, keepdims=True) * TO_EXP2
            weights = jnp.where(causal, jnp.exp2(fresh * TO_EXP2 - peak), 0.0)
            total = weights
            part = jnp.dot(
                weights.astype(BF16), padded(new_values[:, lanes[i]]), preferred_element_type=F32
            )
            for b in range(own // BLK):
                span = slice(b * BLK, (b + 1) * BLK)
                weights = jnp.exp2(scores[i, :, span] * TO_EXP2 - peak)
                for v in range(BLK // HEAD_DIM):
                    total = total + weights[:, v * HEAD_DIM : (v + 1) * HEAD_DIM]
                product = jnp.dot(
                    weights.astype(BF16), codes[r, i, span, :], preferred_element_type=F32
                )
                part = part + product * scales[head_of(r, i), b]
            total = jnp.sum(total, axis=1, keepdims=True)
            keep = mine if i == 0 else theirs
            keep[r, 0] = part
            keep[r, 1] = jnp.where(column < HALF, peak, total)
            if i == 1:
                pair_copy(r).start()
        hook(whole_product)
        return 0

    partial[...] = jnp.zeros_like(partial)
    lax.fori_loop(0, rounds, one_round, 0)
    final = rounds - 1
    combine(final)
    for step in range(levels - 1):
        relay(final, step)
    collect(final)
    half_rows = members * Q_TOK // 2
    half_of = lambda n: pl.ds(pl.multiple_of(n * half_rows, half_rows), half_rows)
    multiply(final, half_of(other))
    last = pltpu.make_async_remote_copy(
        src_ref=partial.at[half_of(other)], dst_ref=got_partial, send_sem=last_send,
        recv_sem=last_recv, device_id=(me, other), device_id_type=MESH,
    )
    last.start()
    multiply(final, half_of(at))
    last.wait()
    out[...] = partial[half_of(at)] + got_partial[...]


def body(lengths, latents, codes, scales, queries, new_keys, new_values, key_factor, out_weight):
    own, rank = latents.shape[1:]
    cosine, sine = rope_tables(own * lax.axis_size("kv"))
    members = lax.axis_size("group")
    levels = members.bit_length() - 1
    assert members == 2**levels and lax.axis_size("kv") == 2
    depth, columns = out_weight.shape
    rounds = KV_HEADS // 2
    count = members * Q_TOK
    pieces = 4
    anywhere = pl.BlockSpec(memory_space=pl.ANY)
    scalar = pl.BlockSpec(memory_space=pltpu.SMEM)
    near = pl.BlockSpec(memory_space=pltpu.VMEM)
    dma = pltpu.SemaphoreType.DMA
    return pl.pallas_call(
        step_kernel,
        out_shape=jax.ShapeDtypeStruct((count // 2, columns), F32),
        in_specs=[scalar, scalar] + [anywhere] * 4 + [near] * 4 + [anywhere],
        out_specs=near,
        scratch_shapes=[
            pltpu.VMEM((rank, own), BF16),
            pltpu.VMEM((rounds, PAIR, own, HEAD_DIM), BF16),
            pltpu.VMEM((HALF, own), F32),
            pltpu.VMEM((HALF, own), F32),
            pltpu.VMEM((depth, columns), BF16),
            pltpu.VMEM((PAIR, ROWS, own), F32),
            pltpu.VMEM((rounds, 2, ROWS, HEAD_DIM), F32),
            pltpu.VMEM((rounds, 2, ROWS, HEAD_DIM), F32),
            pltpu.VMEM((rounds, 2, ROWS, HEAD_DIM), F32),
            pltpu.VMEM((rounds, 2, *[2] * levels, ROWS // 2, HEAD_DIM), BF16),
            pltpu.VMEM((count, GROUPS * HEAD_DIM), BF16),
            pltpu.VMEM((count, columns), F32),
            pltpu.VMEM((count // 2, columns), F32),
            dma((3, pieces)),
            dma((rounds, PAIR)),
            dma,
            dma((rounds,)),
            dma((rounds,)),
            dma,
            dma,
            dma((rounds, 2, levels)),
            dma((rounds, 2, levels)),
        ],
        compiler_params=pltpu.CompilerParams(
            collective_id=0, has_side_effects=True, vmem_limit_bytes=56 * 1024 * 1024
        ),
        name="decode_step",
    )(lengths, scales[0].astype(F32).T, latents[0].T, codes[0], jnp.asarray(cosine),
      jnp.asarray(sine), queries[0], new_keys[0], new_values[0], key_factor, out_weight)


def solution(mesh):
    placed = (
        P("group"),
        P("group", "kv", None),
        P("group", "kv", None),
        P("group", "kv", None),
        P("group", None, None),
        P("group", None, None),
        P("group", None, None),
        P(),
        P("kv", "group"),
    )
    return jax.shard_map(
        body, mesh=mesh, in_specs=placed, out_specs=P("kv", "group"), check_vma=False
    )
```

```python
import math

import jax
import jax.numpy as jnp
import numpy as np
from jax import lax
from jax.experimental import pallas as pl
from jax.experimental.pallas import tpu as pltpu
from jax.sharding import PartitionSpec as P

HEADS = 64
KV_HEADS = 8
GROUPS = HEADS // KV_HEADS
HEAD_DIM = 128
HALF = HEAD_DIM // 2
BLK = 256
Q_TOK = 8
ROWS = Q_TOK * GROUPS
PAIR = 2
CHUNK = 512
ROPE_BASE = 500000.0
NEG_FILL = -1e30
TO_EXP2 = math.log2(math.e) / math.sqrt(HEAD_DIM)
MESH = pl.DeviceIdType.MESH
F32 = jnp.float32
BF16 = jnp.bfloat16


def rope_tables(ctx):
    exponent = -(np.arange(HALF, dtype=np.float64) * 2.0) / HEAD_DIM
    frequency = (ROPE_BASE**exponent).astype(np.float32)
    angles = frequency[:, None] * np.arange(ctx, dtype=np.float32)[None, :]
    angles = angles.astype(np.float64)
    return np.cos(angles).astype(np.float32), np.sin(angles).astype(np.float32)


def stacked_rows(block):
    wide = block.astype(F32)
    return jnp.concatenate(
        [wide[:, g * HEAD_DIM : (g + 1) * HEAD_DIM] for g in range(GROUPS)], axis=0
    ).astype(BF16)


def padded(block):
    wide = block.astype(F32)
    blank = jnp.zeros((HEAD_DIM - Q_TOK, HEAD_DIM), F32)
    return jnp.concatenate([wide, blank], axis=0).astype(BF16)


def step_kernel(
    length, latents_hbm, codes_hbm, cosine_hbm, sine_hbm, scales_in, queries, new_keys,
    new_values, factor, weight_hbm, out,
    latents, codes, cosine, sine, weight, scales, scores, mine, theirs, got, buffer, rows, partial,
    got_partial,
    piece_sem, codes_sem, weight_sem, pair_send, pair_recv, last_send, last_recv,
    column_send, column_recv, plane_send, plane_recv,
):
    at = lax.axis_index("kv")
    other = 1 - at
    me = lax.axis_index("group")
    own = latents.shape[1]
    base = at * own
    rounds = buffer.shape[0]
    plane, floors = buffer.shape[1:3]
    members = plane * floors
    floor, place = me // plane, me % plane
    above = [((floor + d) % floors) * plane + place for d in range(1, floors)]
    beside = [floor * plane + (place + d) % plane for d in range(1, plane)]
    pieces = piece_sem.shape[1]
    wide = own // pieces

    def piece_copies(n):
        span = pl.ds(n * wide, wide)
        there = pl.ds(pl.multiple_of(base + n * wide, wide), wide)
        return [
            pltpu.make_async_copy(latents_hbm.at[:, span], latents.at[:, span], piece_sem.at[0, n]),
            pltpu.make_async_copy(cosine_hbm.at[:, there], cosine.at[:, span], piece_sem.at[1, n]),
            pltpu.make_async_copy(sine_hbm.at[:, there], sine.at[:, span], piece_sem.at[2, n]),
        ]

    def head_of(r, i):
        return (at if i == 0 else other) * rounds + r

    def codes_copies(r):
        result = []
        for i in range(PAIR):
            lanes = pl.ds(pl.multiple_of(head_of(r, i) * HEAD_DIM, HEAD_DIM), HEAD_DIM)
            result.append(
                pltpu.make_async_copy(codes_hbm.at[:, lanes], codes.at[r, i], codes_sem.at[r, i])
            )
        return result

    load = pltpu.make_async_copy(weight_hbm, weight, weight_sem)
    for n in range(pieces):
        for copy in piece_copies(n):
            copy.start()
    for r in range(rounds):
        for copy in codes_copies(r):
            copy.start()
    load.start()

    barrier = pltpu.get_barrier_semaphore()
    pl.semaphore_signal(barrier, inc=1, device_id=(me, other), device_id_type=MESH)
    for peer in above + beside:
        pl.semaphore_signal(barrier, inc=1, device_id=(peer, at), device_id_type=MESH)
    pl.semaphore_wait(barrier, len(above) + len(beside) + 1)
    scales[...] = scales_in[...].astype(F32)

    def pair_copy(r):
        return pltpu.make_async_remote_copy(
            src_ref=theirs.at[r], dst_ref=got.at[r], send_sem=pair_send.at[r],
            recv_sem=pair_recv.at[r], device_id=(me, other), device_id_type=MESH,
        )

    def column_copies(r):
        block = buffer.at[r, place, floor]
        return [
            pltpu.make_async_remote_copy(
                src_ref=block, dst_ref=block, send_sem=column_send.at[r, d],
                recv_sem=column_recv.at[r, d], device_id=(peer, at), device_id_type=MESH,
            )
            for d, peer in enumerate(above)
        ]

    def plane_copies(r):
        block = buffer.at[r, place]
        return [
            pltpu.make_async_remote_copy(
                src_ref=block, dst_ref=block, send_sem=plane_send.at[r, d],
                recv_sem=plane_recv.at[r, d], device_id=(peer, at), device_id_type=MESH,
            )
            for d, peer in enumerate(beside)
        ]

    def combine(r):
        pair_copy(r).wait()
        mine_stat, their_stat = mine[r, 1], got[r, 1]
        mine_peak, mine_total = mine_stat[:, :1], mine_stat[:, HALF : HALF + 1]
        their_peak, their_total = their_stat[:, :1], their_stat[:, HALF : HALF + 1]
        peak = jnp.maximum(mine_peak, their_peak)
        mine_scale, their_scale = jnp.exp2(mine_peak - peak), jnp.exp2(their_peak - peak)
        total = mine_total * mine_scale + their_total * their_scale
        joined = (mine[r, 0] * mine_scale + got[r, 0] * their_scale) / total
        buffer[r, place, floor] = joined.astype(BF16)
        for copy in column_copies(r):
            copy.start()

    def spread(r):
        for copy in column_copies(r):
            copy.wait()
        for copy in plane_copies(r):
            copy.start()

    def collect(r):
        for copy in plane_copies(r):
            copy.wait()
        for z in range(floors):
            block = buffer[r, :, z].astype(F32)
            for g in range(GROUPS):
                piece = block[:, g * Q_TOK : (g + 1) * Q_TOK, :].reshape(plane * Q_TOK, HEAD_DIM)
                rows[
                    z * plane * Q_TOK : (z + 1) * plane * Q_TOK,
                    g * HEAD_DIM : (g + 1) * HEAD_DIM,
                ] = piece.astype(BF16)

    depth = GROUPS * HEAD_DIM

    def multiply(r, span):
        layer = weight[pl.ds(pl.multiple_of(r * depth, depth), depth), :]
        partial[span, :] += jnp.dot(rows[span, :], layer, preferred_element_type=F32)

    def whole_product(r):
        collect(r)

        @pl.when(r == 0)
        def _():
            load.wait()

        multiply(r, slice(None))

    column = lax.broadcasted_iota(jnp.int32, (ROWS, HEAD_DIM), 1)
    token = lax.broadcasted_iota(jnp.int32, (ROWS, HEAD_DIM), 0) % Q_TOK
    causal = jnp.logical_and(column <= token, at == 0)
    limit = length[0] - base

    def one_round(r, _):
        def hook(action, back):
            @pl.when(r >= back)
            def _():
                action(r - back)

        lanes = [
            pl.ds(pl.multiple_of(head_of(r, i) * HEAD_DIM, HEAD_DIM), HEAD_DIM)
            for i in range(PAIR)
        ]
        turned = jnp.concatenate(
            [factor[:, lanes[i]].astype(F32).T for i in range(PAIR)], axis=0
        ).astype(BF16)
        query = [
            stacked_rows(queries[:, pl.ds(pl.multiple_of(head_of(r, i) * depth, depth), depth)])
            for i in range(PAIR)
        ]
        factors = [scales[pl.ds(head_of(r, i), 1), :] for i in range(PAIR)]
        tops = [jnp.full((ROWS, HEAD_DIM), NEG_FILL, F32) for _ in range(PAIR)]
        for c in range(own // CHUNK):
            span = slice(c * CHUNK, (c + 1) * CHUNK)
            if c * CHUNK % wide == 0:

                @pl.when(r == 0)
                def _(n=c * CHUNK // wide):
                    for copy in piece_copies(n):
                        copy.wait()

            keys = jnp.dot(turned, latents[:, span], preferred_element_type=F32)
            cos, sin = cosine[:, span], sine[:, span]
            valid = c * CHUNK + lax.broadcasted_iota(jnp.int32, (1, CHUNK), 1) < limit
            for i in range(PAIR):
                low = keys[i * HEAD_DIM : i * HEAD_DIM + HALF]
                high = keys[i * HEAD_DIM + HALF : (i + 1) * HEAD_DIM]
                rotated = jnp.concatenate(
                    [low * cos - high * sin, high * cos + low * sin], axis=0
                ).astype(BF16)
                score = jnp.dot(query[i], rotated, preferred_element_type=F32)
                score = jnp.where(valid, score, NEG_FILL)
                scores[i, :, span] = score
                for v in range(CHUNK // HEAD_DIM):
                    tops[i] = jnp.maximum(tops[i], score[:, v * HEAD_DIM : (v + 1) * HEAD_DIM])
            if c == 3:
                hook(whole_product, 2)
            if c == own // CHUNK - 2:
                hook(combine, 1)
        for copy in codes_copies(r):
            copy.wait()
        for i in (1, 0):
            fresh = lax.dot_general(
                query[i], padded(new_keys[:, lanes[i]]), (((1,), (1,)), ((), ())),
                preferred_element_type=F32,
            )
            fresh = jnp.where(causal, fresh, NEG_FILL)
            peak = jnp.max(jnp.maximum(tops[i], fresh), axis=1, keepdims=True) * TO_EXP2
            weights = jnp.where(causal, jnp.exp2(fresh * TO_EXP2 - peak), 0.0)
            total = weights
            part = jnp.dot(
                weights.astype(BF16), padded(new_values[:, lanes[i]]), preferred_element_type=F32
            )
            for b in range(own // BLK):
                span = slice(b * BLK, (b + 1) * BLK)
                weights = jnp.exp2(scores[i, :, span] * TO_EXP2 - peak)
                for v in range(BLK // HEAD_DIM):
                    total = total + weights[:, v * HEAD_DIM : (v + 1) * HEAD_DIM]
                product = jnp.dot(
                    weights.astype(BF16), codes[r, i, span, :], preferred_element_type=F32
                )
                part = part + product * factors[i][:, b : b + 1]
            total = jnp.sum(total, axis=1, keepdims=True)
            keep = mine if i == 0 else theirs
            keep[r, 0] = part
            keep[r, 1] = jnp.where(column < HALF, peak, total)
            if i == 1:
                pair_copy(r).start()
        hook(spread, 1)
        return 0

    partial[...] = jnp.zeros_like(partial)
    lax.fori_loop(0, rounds, one_round, 0)
    final = rounds - 1
    combine(final)
    whole_product(final - 1)
    spread(final)
    collect(final)
    half_rows = members * Q_TOK // 2
    half_of = lambda n: pl.ds(pl.multiple_of(n * half_rows, half_rows), half_rows)
    multiply(final, half_of(other))
    last = pltpu.make_async_remote_copy(
        src_ref=partial.at[half_of(other)], dst_ref=got_partial, send_sem=last_send,
        recv_sem=last_recv, device_id=(me, other), device_id_type=MESH,
    )
    last.start()
    multiply(final, half_of(at))
    last.wait()
    out[...] = partial[half_of(at)] + got_partial[...]


def body(lengths, latents, codes, scales, queries, new_keys, new_values, key_factor, out_weight):
    own, rank = latents.shape[1:]
    cosine, sine = rope_tables(own * lax.axis_size("kv"))
    members = lax.axis_size("group")
    floors = 4 if members % 4 == 0 else 1
    plane = members // floors
    depth, columns = out_weight.shape
    rounds = KV_HEADS // 2
    count = members * Q_TOK
    pieces = 4
    anywhere = pl.BlockSpec(memory_space=pl.ANY)
    scalar = pl.BlockSpec(memory_space=pltpu.SMEM)
    near = pl.BlockSpec(memory_space=pltpu.VMEM)
    dma = pltpu.SemaphoreType.DMA
    return pl.pallas_call(
        step_kernel,
        out_shape=jax.ShapeDtypeStruct((count // 2, columns), F32),
        in_specs=[scalar] + [anywhere] * 4 + [near] * 5 + [anywhere],
        out_specs=near,
        scratch_shapes=[
            pltpu.VMEM((rank, own), BF16),
            pltpu.VMEM((rounds, PAIR, own, HEAD_DIM), BF16),
            pltpu.VMEM((HALF, own), F32),
            pltpu.VMEM((HALF, own), F32),
            pltpu.VMEM((depth, columns), BF16),
            pltpu.VMEM(scales.shape[:0:-1], F32),
            pltpu.VMEM((PAIR, ROWS, own), F32),
            pltpu.VMEM((rounds, 2, ROWS, HEAD_DIM), F32),
            pltpu.VMEM((rounds, 2, ROWS, HEAD_DIM), F32),
            pltpu.VMEM((rounds, 2, ROWS, HEAD_DIM), F32),
            pltpu.VMEM((rounds, plane, floors, ROWS, HEAD_DIM), BF16),
            pltpu.VMEM((count, GROUPS * HEAD_DIM), BF16),
            pltpu.VMEM((count, columns), F32),
            pltpu.VMEM((count // 2, columns), F32),
            dma((3, pieces)),
            dma((rounds, PAIR)),
            dma,
            dma((rounds,)),
            dma((rounds,)),
            dma,
            dma,
            dma((rounds, max(floors - 1, 1))),
            dma((rounds, max(floors - 1, 1))),
            dma((rounds, max(plane - 1, 1))),
            dma((rounds, max(plane - 1, 1))),
        ],
        compiler_params=pltpu.CompilerParams(
            collective_id=0, has_side_effects=True, vmem_limit_bytes=54 * 1024 * 1024
        ),
        name="decode_step",
    )(lengths, latents[0].T, codes[0], jnp.asarray(cosine), jnp.asarray(sine), scales[0].T,
      queries[0], new_keys[0], new_values[0], key_factor, out_weight)


def solution(mesh):
    placed = (
        P("group"),
        P("group", "kv", None),
        P("group", "kv", None),
        P("group", "kv", None),
        P("group", None, None),
        P("group", None, None),
        P("group", None, None),
        P(),
        P("kv", "group"),
    )
    return jax.shard_map(
        body, mesh=mesh, in_specs=placed, out_specs=P("kv", "group"), check_vma=False
    )
```

```python
import math

import jax
import jax.numpy as jnp
import numpy as np
from jax import lax
from jax.experimental import pallas as pl
from jax.experimental.pallas import tpu as pltpu
from jax.sharding import PartitionSpec as P

HEADS = 64
KV_HEADS = 8
GROUPS = HEADS // KV_HEADS
HEAD_DIM = 128
HALF = HEAD_DIM // 2
BLK = 256
Q_TOK = 8
ROWS = Q_TOK * GROUPS
PAIR = 2
CHUNK = 512
ROPE_BASE = 500000.0
NEG_FILL = -1e30
TO_EXP2 = math.log2(math.e) / math.sqrt(HEAD_DIM)
MESH = pl.DeviceIdType.MESH
F32 = jnp.float32
BF16 = jnp.bfloat16


def rope_tables(ctx):
    exponent = -(np.arange(HALF, dtype=np.float64) * 2.0) / HEAD_DIM
    frequency = (ROPE_BASE**exponent).astype(np.float32)
    angles = frequency[:, None] * np.arange(ctx, dtype=np.float32)[None, :]
    angles = angles.astype(np.float64)
    return np.cos(angles).astype(np.float32), np.sin(angles).astype(np.float32)


def stacked_rows(block):
    wide = block.astype(F32)
    return jnp.concatenate(
        [wide[:, g * HEAD_DIM : (g + 1) * HEAD_DIM] for g in range(GROUPS)], axis=0
    ).astype(BF16)


def padded(block):
    wide = block.astype(F32)
    blank = jnp.zeros((HEAD_DIM - Q_TOK, HEAD_DIM), F32)
    return jnp.concatenate([wide, blank], axis=0).astype(BF16)


def step_kernel(
    length, latents_hbm, codes_hbm, cosine_hbm, sine_hbm, scales_hbm, queries_hbm,
    new_keys_hbm, new_values_hbm, factor_hbm, weight_hbm, out,
    scales_in, queries, late_keys, late_values, factor,
    latents, codes, cosine, sine, weight, scales, scores, mine, theirs, got, buffer, rows, partial,
    got_partial,
    small_sem, piece_sem, codes_sem, weight_sem, pair_send, pair_recv, last_send, last_recv,
    column_send, column_recv, plane_send, plane_recv,
):
    at = lax.axis_index("kv")
    other = 1 - at
    me = lax.axis_index("group")
    own = latents.shape[1]
    base = at * own
    rounds = buffer.shape[0]
    plane, floors = buffer.shape[1:3]
    members = plane * floors
    floor, place = me // plane, me % plane
    above = [((floor + d) % floors) * plane + place for d in range(1, floors)]
    beside = [floor * plane + (place + d) % plane for d in range(1, plane)]
    pieces = piece_sem.shape[1]
    wide = own // pieces

    def piece_copies(n):
        span = pl.ds(n * wide, wide)
        there = pl.ds(pl.multiple_of(base + n * wide, wide), wide)
        return [
            pltpu.make_async_copy(latents_hbm.at[:, span], latents.at[:, span], piece_sem.at[0, n]),
            pltpu.make_async_copy(cosine_hbm.at[:, there], cosine.at[:, span], piece_sem.at[1, n]),
            pltpu.make_async_copy(sine_hbm.at[:, there], sine.at[:, span], piece_sem.at[2, n]),
        ]

    def head_of(r, i):
        return (at if i == 0 else other) * rounds + r

    def codes_copies(r):
        result = []
        for i in range(PAIR):
            lanes = pl.ds(pl.multiple_of(head_of(r, i) * HEAD_DIM, HEAD_DIM), HEAD_DIM)
            result.append(
                pltpu.make_async_copy(
                    codes_hbm.at[:, lanes],
                    codes.at[r, :, pl.ds(i * HEAD_DIM, HEAD_DIM)],
                    codes_sem.at[r, i],
                )
            )
        return result

    load = pltpu.make_async_copy(weight_hbm, weight, weight_sem)
    small = [
        pltpu.make_async_copy(source, target, small_sem.at[n])
        for n, (source, target) in enumerate((
            (factor_hbm, factor),
            (queries_hbm, queries),
            (new_keys_hbm, late_keys),
            (new_values_hbm, late_values),
            (scales_hbm, scales_in),
        ))
    ]
    for copy in small:
        copy.start()
    for n in range(pieces):
        for copy in piece_copies(n):
            copy.start()
    for r in range(rounds):
        for copy in codes_copies(r):
            copy.start()
    load.start()

    barrier = pltpu.get_barrier_semaphore()
    pl.semaphore_signal(barrier, inc=1, device_id=(me, other), device_id_type=MESH)
    for peer in above + beside:
        pl.semaphore_signal(barrier, inc=1, device_id=(peer, at), device_id_type=MESH)
    pl.semaphore_wait(barrier, len(above) + len(beside) + 1)
    for copy in small:
        copy.wait()
    scales[...] = scales_in[...].astype(F32)

    def pair_copy(r):
        return pltpu.make_async_remote_copy(
            src_ref=theirs.at[r], dst_ref=got.at[r], send_sem=pair_send.at[r],
            recv_sem=pair_recv.at[r], device_id=(me, other), device_id_type=MESH,
        )

    def column_copies(r):
        block = buffer.at[r, place, floor]
        return [
            pltpu.make_async_remote_copy(
                src_ref=block, dst_ref=block, send_sem=column_send.at[r, d],
                recv_sem=column_recv.at[r, d], device_id=(peer, at), device_id_type=MESH,
            )
            for d, peer in enumerate(above)
        ]

    def plane_copies(r):
        block = buffer.at[r, place]
        return [
            pltpu.make_async_remote_copy(
                src_ref=block, dst_ref=block, send_sem=plane_send.at[r, d],
                recv_sem=plane_recv.at[r, d], device_id=(peer, at), device_id_type=MESH,
            )
            for d, peer in enumerate(beside)
        ]

    def combine(r):
        pair_copy(r).wait()
        mine_stat, their_stat = mine[r, 1], got[r, 1]
        mine_peak, mine_total = mine_stat[:, :1], mine_stat[:, HALF : HALF + 1]
        their_peak, their_total = their_stat[:, :1], their_stat[:, HALF : HALF + 1]
        peak = jnp.maximum(mine_peak, their_peak)
        mine_scale, their_scale = jnp.exp2(mine_peak - peak), jnp.exp2(their_peak - peak)
        total = mine_total * mine_scale + their_total * their_scale
        joined = (mine[r, 0] * mine_scale + got[r, 0] * their_scale) / total
        buffer[r, place, floor] = joined.astype(BF16)
        for copy in column_copies(r):
            copy.start()

    def spread(r):
        for copy in column_copies(r):
            copy.wait()
        for copy in plane_copies(r):
            copy.start()

    def collect(r):
        for copy in plane_copies(r):
            copy.wait()
        for z in range(floors):
            block = buffer[r, :, z].astype(F32)
            for g in range(GROUPS):
                piece = block[:, g * Q_TOK : (g + 1) * Q_TOK, :].reshape(plane * Q_TOK, HEAD_DIM)
                rows[
                    z * plane * Q_TOK : (z + 1) * plane * Q_TOK,
                    g * HEAD_DIM : (g + 1) * HEAD_DIM,
                ] = piece.astype(BF16)

    depth = GROUPS * HEAD_DIM

    def multiply(r, span):
        layer = weight[pl.ds(pl.multiple_of(r * depth, depth), depth), :]
        partial[span, :] += jnp.dot(rows[span, :], layer, preferred_element_type=F32)

    def whole_product(r):
        collect(r)

        @pl.when(r == 0)
        def _():
            load.wait()

        multiply(r, slice(None))

    column = lax.broadcasted_iota(jnp.int32, (ROWS, HEAD_DIM), 1)
    token = lax.broadcasted_iota(jnp.int32, (ROWS, HEAD_DIM), 0) % Q_TOK
    causal = jnp.logical_and(column <= token, at == 0)
    limit = length[0] - base

    def one_round(r, _):
        def hook(action, back):
            @pl.when(r >= back)
            def _():
                action(r - back)

        lanes = [
            pl.ds(pl.multiple_of(head_of(r, i) * HEAD_DIM, HEAD_DIM), HEAD_DIM)
            for i in range(PAIR)
        ]
        turned = jnp.concatenate(
            [factor[:, lanes[i]].astype(F32).T for i in range(PAIR)], axis=0
        ).astype(BF16)
        query = [
            stacked_rows(queries[:, pl.ds(pl.multiple_of(head_of(r, i) * depth, depth), depth)])
            for i in range(PAIR)
        ]
        factors = [scales[pl.ds(head_of(r, i), 1), :] for i in range(PAIR)]
        tops = [jnp.full((ROWS, HEAD_DIM), NEG_FILL, F32) for _ in range(PAIR)]
        for c in range(own // CHUNK):
            span = slice(c * CHUNK, (c + 1) * CHUNK)
            if c * CHUNK % wide == 0:

                @pl.when(r == 0)
                def _(n=c * CHUNK // wide):
                    for copy in piece_copies(n):
                        copy.wait()

            keys = jnp.dot(turned, latents[:, span], preferred_element_type=F32)
            cos, sin = cosine[:, span], sine[:, span]
            valid = c * CHUNK + lax.broadcasted_iota(jnp.int32, (1, CHUNK), 1) < limit
            for i in range(PAIR):
                low = keys[i * HEAD_DIM : i * HEAD_DIM + HALF]
                high = keys[i * HEAD_DIM + HALF : (i + 1) * HEAD_DIM]
                rotated = jnp.concatenate(
                    [low * cos - high * sin, high * cos + low * sin], axis=0
                ).astype(BF16)
                score = jnp.dot(query[i], rotated, preferred_element_type=F32)
                score = jnp.where(valid, score, NEG_FILL)
                scores[i, :, span] = score
                for v in range(CHUNK // HEAD_DIM):
                    tops[i] = jnp.maximum(tops[i], score[:, v * HEAD_DIM : (v + 1) * HEAD_DIM])
            if c == 1:
                hook(combine, 1)
            if c == own // CHUNK - 3:
                hook(whole_product, 2)
        hook(spread, 1)
        for copy in codes_copies(r):
            copy.wait()
        peaks, totals, parts = [], [], []
        for i in range(PAIR):
            fresh = lax.dot_general(
                query[i], padded(late_keys[:, lanes[i]]), (((1,), (1,)), ((), ())),
                preferred_element_type=F32,
            )
            fresh = jnp.where(causal, fresh, NEG_FILL)
            peak = jnp.max(jnp.maximum(tops[i], fresh), axis=1, keepdims=True) * TO_EXP2
            peaks.append(jnp.broadcast_to(peak, (ROWS, BLK)))
            weights = jnp.where(causal, jnp.exp2(fresh * TO_EXP2 - peak), 0.0)
            totals.append(weights)
            parts.append(
                jnp.dot(
                    weights.astype(BF16), padded(late_values[:, lanes[i]]),
                    preferred_element_type=F32,
                )
            )
        for b in range(own // BLK):
            span = slice(b * BLK, (b + 1) * BLK)
            both = []
            for i in range(PAIR):
                weights = jnp.exp2(scores[i, :, span] * TO_EXP2 - peaks[i])
                for v in range(BLK // HEAD_DIM):
                    totals[i] = totals[i] + weights[:, v * HEAD_DIM : (v + 1) * HEAD_DIM]
                both.append(weights.astype(BF16))
            product = jnp.dot(
                jnp.concatenate(both, axis=0), codes[r, span, :], preferred_element_type=F32
            )
            for i in range(PAIR):
                own_part = product[
                    i * ROWS : (i + 1) * ROWS, i * HEAD_DIM : (i + 1) * HEAD_DIM
                ]
                parts[i] = parts[i] + own_part * factors[i][:, b : b + 1]
        for i, keep in ((1, theirs), (0, mine)):
            total = jnp.sum(totals[i], axis=1, keepdims=True)
            keep[r, 0] = parts[i]
            keep[r, 1] = jnp.where(column < HALF, peaks[i][:, :HEAD_DIM], total)
            if i == 1:
                pair_copy(r).start()
        return 0

    partial[...] = jnp.zeros_like(partial)
    lax.fori_loop(0, rounds, one_round, 0)
    final = rounds - 1
    combine(final)
    whole_product(final - 1)
    spread(final)
    collect(final)
    half_rows = members * Q_TOK // 2
    half_of = lambda n: pl.ds(pl.multiple_of(n * half_rows, half_rows), half_rows)
    multiply(final, half_of(other))
    last = pltpu.make_async_remote_copy(
        src_ref=partial.at[half_of(other)], dst_ref=got_partial, send_sem=last_send,
        recv_sem=last_recv, device_id=(me, other), device_id_type=MESH,
    )
    last.start()
    multiply(final, half_of(at))
    last.wait()
    out[...] = partial[half_of(at)] + got_partial[...]


def body(lengths, latents, codes, scales, queries, new_keys, new_values, key_factor, out_weight):
    own, rank = latents.shape[1:]
    cosine, sine = rope_tables(own * lax.axis_size("kv"))
    members = lax.axis_size("group")
    floors = 4 if members % 4 == 0 else 1
    plane = members // floors
    depth, columns = out_weight.shape
    rounds = KV_HEADS // 2
    count = members * Q_TOK
    pieces = 4
    anywhere = pl.BlockSpec(memory_space=pl.ANY)
    scalar = pl.BlockSpec(memory_space=pltpu.SMEM)
    near = pl.BlockSpec(memory_space=pltpu.VMEM)
    dma = pltpu.SemaphoreType.DMA
    return pl.pallas_call(
        step_kernel,
        out_shape=jax.ShapeDtypeStruct((count // 2, columns), F32),
        in_specs=[scalar] + [anywhere] * 10,
        out_specs=near,
        scratch_shapes=[
            pltpu.VMEM(scales.shape[:0:-1], BF16),
            pltpu.VMEM(queries.shape[1:], BF16),
            pltpu.VMEM(new_keys.shape[1:], BF16),
            pltpu.VMEM(new_values.shape[1:], BF16),
            pltpu.VMEM(key_factor.shape, BF16),
            pltpu.VMEM((rank, own), BF16),
            pltpu.VMEM((rounds, own, PAIR * HEAD_DIM), BF16),
            pltpu.VMEM((HALF, own), F32),
            pltpu.VMEM((HALF, own), F32),
            pltpu.VMEM((depth, columns), BF16),
            pltpu.VMEM(scales.shape[:0:-1], F32),
            pltpu.VMEM((PAIR, ROWS, own), F32),
            pltpu.VMEM((rounds, 2, ROWS, HEAD_DIM), F32),
            pltpu.VMEM((rounds, 2, ROWS, HEAD_DIM), F32),
            pltpu.VMEM((rounds, 2, ROWS, HEAD_DIM), F32),
            pltpu.VMEM((rounds, plane, floors, ROWS, HEAD_DIM), BF16),
            pltpu.VMEM((count, GROUPS * HEAD_DIM), BF16),
            pltpu.VMEM((count, columns), F32),
            pltpu.VMEM((count // 2, columns), F32),
            dma((5,)),
            dma((3, pieces)),
            dma((rounds, PAIR)),
            dma,
            dma((rounds,)),
            dma((rounds,)),
            dma,
            dma,
            dma((rounds, max(floors - 1, 1))),
            dma((rounds, max(floors - 1, 1))),
            dma((rounds, max(plane - 1, 1))),
            dma((rounds, max(plane - 1, 1))),
        ],
        compiler_params=pltpu.CompilerParams(
            collective_id=0, has_side_effects=True, vmem_limit_bytes=107 * 512 * 1024
        ),
        name="decode_step",
    )(lengths, latents[0].T, codes[0], jnp.asarray(cosine), jnp.asarray(sine), scales[0].T,
      queries[0], new_keys[0], new_values[0], key_factor, out_weight)


def solution(mesh):
    placed = (
        P("group"),
        P("group", "kv", None),
        P("group", "kv", None),
        P("group", "kv", None),
        P("group", None, None),
        P("group", None, None),
        P("group", None, None),
        P(),
        P("kv", "group"),
    )
    return jax.shard_map(
        body, mesh=mesh, in_specs=placed, out_specs=P("kv", "group"), check_vma=False
    )
```

```python
import math

import jax
import jax.numpy as jnp
import numpy as np
from jax import lax
from jax.experimental import pallas as pl
from jax.experimental.pallas import tpu as pltpu
from jax.sharding import PartitionSpec as P

HEADS = 64
KV_HEADS = 8
GROUPS = HEADS // KV_HEADS
HEAD_DIM = 128
HALF = HEAD_DIM // 2
BLK = 256
Q_TOK = 8
ROWS = Q_TOK * GROUPS
PAIR = 2
CHUNK = 512
ROPE_BASE = 500000.0
NEG_FILL = -1e30
TO_EXP2 = math.log2(math.e) / math.sqrt(HEAD_DIM)
MESH = pl.DeviceIdType.MESH
F32 = jnp.float32
BF16 = jnp.bfloat16


def rope_tables(ctx):
    exponent = -(np.arange(HALF, dtype=np.float64) * 2.0) / HEAD_DIM
    frequency = (ROPE_BASE**exponent).astype(np.float32)
    angles = frequency[:, None] * np.arange(ctx, dtype=np.float32)[None, :]
    angles = angles.astype(np.float64)
    return np.cos(angles).astype(np.float32), np.sin(angles).astype(np.float32)


def stacked_rows(block):
    wide = block.astype(F32)
    return jnp.concatenate(
        [wide[:, g * HEAD_DIM : (g + 1) * HEAD_DIM] for g in range(GROUPS)], axis=0
    ).astype(BF16)


def padded(block):
    wide = block.astype(F32)
    blank = jnp.zeros((HEAD_DIM - Q_TOK, HEAD_DIM), F32)
    return jnp.concatenate([wide, blank], axis=0).astype(BF16)


def step_kernel(
    length, latents_hbm, codes_hbm, cosine_hbm, sine_hbm, scales_hbm, queries_hbm,
    new_keys_hbm, new_values_hbm, factor_hbm, weight_hbm, out,
    scales_in, queries, late_keys, late_values, factor,
    latents, codes, cosine, sine, weight, scales, scores, mine, theirs, got, buffer, rows, partial,
    got_partial,
    small_sem, piece_sem, codes_sem, weight_sem, pair_send, pair_recv, last_send, last_recv,
    column_send, column_recv, plane_send, plane_recv,
):
    at = lax.axis_index("kv")
    other = 1 - at
    me = lax.axis_index("group")
    own = latents.shape[1]
    base = at * own
    rounds = buffer.shape[0]
    plane, floors = buffer.shape[1:3]
    members = plane * floors
    floor, place = me // plane, me % plane
    above = [((floor + d) % floors) * plane + place for d in range(1, floors)]
    beside = [floor * plane + (place + d) % plane for d in range(1, plane)]
    pieces = piece_sem.shape[1]
    wide = own // pieces

    def piece_copies(n):
        span = pl.ds(n * wide, wide)
        there = pl.ds(pl.multiple_of(base + n * wide, wide), wide)
        return [
            pltpu.make_async_copy(latents_hbm.at[:, span], latents.at[:, span], piece_sem.at[0, n]),
            pltpu.make_async_copy(cosine_hbm.at[:, there], cosine.at[:, span], piece_sem.at[1, n]),
            pltpu.make_async_copy(sine_hbm.at[:, there], sine.at[:, span], piece_sem.at[2, n]),
        ]

    def head_of(r, i):
        return (at if i == 0 else other) * rounds + r

    def codes_copies(r):
        result = []
        for i in range(PAIR):
            lanes = pl.ds(pl.multiple_of(head_of(r, i) * HEAD_DIM, HEAD_DIM), HEAD_DIM)
            result.append(
                pltpu.make_async_copy(
                    codes_hbm.at[:, lanes],
                    codes.at[r, :, pl.ds(i * HEAD_DIM, HEAD_DIM)],
                    codes_sem.at[r, i],
                )
            )
        return result

    load = pltpu.make_async_copy(weight_hbm, weight, weight_sem)
    small = [
        pltpu.make_async_copy(source, target, small_sem.at[n])
        for n, (source, target) in enumerate((
            (factor_hbm, factor),
            (queries_hbm, queries),
            (new_keys_hbm, late_keys),
            (new_values_hbm, late_values),
            (scales_hbm, scales_in),
        ))
    ]
    for copy in small:
        copy.start()
    for n in range(pieces):
        for copy in piece_copies(n):
            copy.start()
    for r in range(rounds):
        for copy in codes_copies(r):
            copy.start()
    load.start()

    barrier = pltpu.get_barrier_semaphore()
    pl.semaphore_signal(barrier, inc=1, device_id=(me, other), device_id_type=MESH)
    for peer in above + beside:
        pl.semaphore_signal(barrier, inc=1, device_id=(peer, at), device_id_type=MESH)
    pl.semaphore_wait(barrier, len(above) + len(beside) + 1)
    for copy in small:
        copy.wait()
    scales[...] = scales_in[...].astype(F32)

    def pair_copy(r):
        return pltpu.make_async_remote_copy(
            src_ref=theirs.at[r], dst_ref=got.at[r], send_sem=pair_send.at[r],
            recv_sem=pair_recv.at[r], device_id=(me, other), device_id_type=MESH,
        )

    def column_copies(r):
        block = buffer.at[r, place, floor]
        return [
            pltpu.make_async_remote_copy(
                src_ref=block, dst_ref=block, send_sem=column_send.at[r, d],
                recv_sem=column_recv.at[r, d], device_id=(peer, at), device_id_type=MESH,
            )
            for d, peer in enumerate(above)
        ]

    def plane_copies(r):
        block = buffer.at[r, place]
        return [
            pltpu.make_async_remote_copy(
                src_ref=block, dst_ref=block, send_sem=plane_send.at[r, d],
                recv_sem=plane_recv.at[r, d], device_id=(peer, at), device_id_type=MESH,
            )
            for d, peer in enumerate(beside)
        ]

    def combine(r):
        pair_copy(r).wait()
        mine_stat, their_stat = mine[r, 1], got[r, 1]
        mine_peak, mine_total = mine_stat[:, :1], mine_stat[:, HALF : HALF + 1]
        their_peak, their_total = their_stat[:, :1], their_stat[:, HALF : HALF + 1]
        peak = jnp.maximum(mine_peak, their_peak)
        mine_scale, their_scale = jnp.exp2(mine_peak - peak), jnp.exp2(their_peak - peak)
        total = mine_total * mine_scale + their_total * their_scale
        joined = (mine[r, 0] * mine_scale + got[r, 0] * their_scale) / total
        buffer[r, place, floor] = joined.astype(BF16)
        for copy in column_copies(r):
            copy.start()

    def spread(r):
        for copy in column_copies(r):
            copy.wait()
        for copy in plane_copies(r):
            copy.start()

    def collect(r):
        for copy in plane_copies(r):
            copy.wait()
        for z in range(floors):
            block = buffer[r, :, z].astype(F32)
            for g in range(GROUPS):
                piece = block[:, g * Q_TOK : (g + 1) * Q_TOK, :].reshape(plane * Q_TOK, HEAD_DIM)
                rows[
                    z * plane * Q_TOK : (z + 1) * plane * Q_TOK,
                    g * HEAD_DIM : (g + 1) * HEAD_DIM,
                ] = piece.astype(BF16)

    depth = GROUPS * HEAD_DIM

    def multiply(r, span):
        layer = weight[pl.ds(pl.multiple_of(r * depth, depth), depth), :]
        partial[span, :] += jnp.dot(rows[span, :], layer, preferred_element_type=F32)

    def whole_product(r):
        collect(r)

        @pl.when(r == 0)
        def _():
            load.wait()

        multiply(r, slice(None))

    column = lax.broadcasted_iota(jnp.int32, (ROWS, HEAD_DIM), 1)
    token = lax.broadcasted_iota(jnp.int32, (ROWS, HEAD_DIM), 0) % Q_TOK
    causal = jnp.logical_and(column <= token, at == 0)
    limit = length[0] - base

    def one_round(r, _):
        def hook(action, back):
            @pl.when(r >= back)
            def _():
                action(r - back)

        lanes = [
            pl.ds(pl.multiple_of(head_of(r, i) * HEAD_DIM, HEAD_DIM), HEAD_DIM)
            for i in range(PAIR)
        ]
        turned = jnp.concatenate(
            [factor[:, lanes[i]].astype(F32).T for i in range(PAIR)], axis=0
        ).astype(BF16)
        query = [
            stacked_rows(queries[:, pl.ds(pl.multiple_of(head_of(r, i) * depth, depth), depth)])
            for i in range(PAIR)
        ]
        factors = [scales[pl.ds(head_of(r, i), 1), :] for i in range(PAIR)]
        tops = [jnp.full((ROWS, HEAD_DIM), NEG_FILL, F32) for _ in range(PAIR)]
        for c in range(own // CHUNK):
            span = slice(c * CHUNK, (c + 1) * CHUNK)
            if c * CHUNK % wide == 0:

                @pl.when(r == 0)
                def _(n=c * CHUNK // wide):
                    for copy in piece_copies(n):
                        copy.wait()

            keys = jnp.dot(turned, latents[:, span], preferred_element_type=F32)
            cos, sin = cosine[:, span], sine[:, span]
            valid = c * CHUNK + lax.broadcasted_iota(jnp.int32, (1, CHUNK), 1) < limit
            for i in range(PAIR):
                low = keys[i * HEAD_DIM : i * HEAD_DIM + HALF]
                high = keys[i * HEAD_DIM + HALF : (i + 1) * HEAD_DIM]
                rotated = jnp.concatenate(
                    [low * cos - high * sin, high * cos + low * sin], axis=0
                ).astype(BF16)
                score = jnp.dot(query[i], rotated, preferred_element_type=F32)
                score = jnp.where(valid, score, NEG_FILL)
                scores[i, :, span] = score
                for v in range(CHUNK // HEAD_DIM):
                    tops[i] = jnp.maximum(tops[i], score[:, v * HEAD_DIM : (v + 1) * HEAD_DIM])
            if c == 1:
                hook(whole_product, 3)
            if c == 3:
                hook(spread, 2)
        hook(combine, 1)
        for copy in codes_copies(r):
            copy.wait()
        peaks, totals, parts = [], [], []
        for i in range(PAIR):
            fresh = lax.dot_general(
                query[i], padded(late_keys[:, lanes[i]]), (((1,), (1,)), ((), ())),
                preferred_element_type=F32,
            )
            fresh = jnp.where(causal, fresh, NEG_FILL)
            peak = jnp.max(jnp.maximum(tops[i], fresh), axis=1, keepdims=True) * TO_EXP2
            peaks.append(jnp.broadcast_to(peak, (ROWS, BLK)))
            weights = jnp.where(causal, jnp.exp2(fresh * TO_EXP2 - peak), 0.0)
            totals.append(weights)
            parts.append(
                jnp.dot(
                    weights.astype(BF16), padded(late_values[:, lanes[i]]),
                    preferred_element_type=F32,
                )
            )
        for b in range(own // BLK):
            span = slice(b * BLK, (b + 1) * BLK)
            both = []
            for i in range(PAIR):
                weights = jnp.exp2(scores[i, :, span] * TO_EXP2 - peaks[i])
                for v in range(BLK // HEAD_DIM):
                    totals[i] = totals[i] + weights[:, v * HEAD_DIM : (v + 1) * HEAD_DIM]
                both.append(weights.astype(BF16))
            product = jnp.dot(
                jnp.concatenate(both, axis=0), codes[r, span, :], preferred_element_type=F32
            )
            for i in range(PAIR):
                own_part = product[
                    i * ROWS : (i + 1) * ROWS, i * HEAD_DIM : (i + 1) * HEAD_DIM
                ]
                parts[i] = parts[i] + own_part * factors[i][:, b : b + 1]
        for i, keep in ((1, theirs), (0, mine)):
            total = jnp.sum(totals[i], axis=1, keepdims=True)
            keep[r, 0] = parts[i]
            keep[r, 1] = jnp.where(column < HALF, peaks[i][:, :HEAD_DIM], total)
            if i == 1:
                pair_copy(r).start()
        return 0

    partial[...] = jnp.zeros_like(partial)
    lax.fori_loop(0, rounds, one_round, 0)
    final = rounds - 1
    combine(final)
    spread(final - 1)
    whole_product(final - 2)
    spread(final)
    whole_product(final - 1)
    collect(final)
    half_rows = members * Q_TOK // 2
    half_of = lambda n: pl.ds(pl.multiple_of(n * half_rows, half_rows), half_rows)
    multiply(final, half_of(other))
    last = pltpu.make_async_remote_copy(
        src_ref=partial.at[half_of(other)], dst_ref=got_partial, send_sem=last_send,
        recv_sem=last_recv, device_id=(me, other), device_id_type=MESH,
    )
    last.start()
    multiply(final, half_of(at))
    last.wait()
    out[...] = partial[half_of(at)] + got_partial[...]


def body(lengths, latents, codes, scales, queries, new_keys, new_values, key_factor, out_weight):
    own, rank = latents.shape[1:]
    cosine, sine = rope_tables(own * lax.axis_size("kv"))
    members = lax.axis_size("group")
    floors = 4 if members % 4 == 0 else 1
    plane = members // floors
    depth, columns = out_weight.shape
    rounds = KV_HEADS // 2
    count = members * Q_TOK
    pieces = 4
    anywhere = pl.BlockSpec(memory_space=pl.ANY)
    scalar = pl.BlockSpec(memory_space=pltpu.SMEM)
    near = pl.BlockSpec(memory_space=pltpu.VMEM)
    dma = pltpu.SemaphoreType.DMA
    return pl.pallas_call(
        step_kernel,
        out_shape=jax.ShapeDtypeStruct((count // 2, columns), F32),
        in_specs=[scalar] + [anywhere] * 10,
        out_specs=near,
        scratch_shapes=[
            pltpu.VMEM(scales.shape[:0:-1], BF16),
            pltpu.VMEM(queries.shape[1:], BF16),
            pltpu.VMEM(new_keys.shape[1:], BF16),
            pltpu.VMEM(new_values.shape[1:], BF16),
            pltpu.VMEM(key_factor.shape, BF16),
            pltpu.VMEM((rank, own), BF16),
            pltpu.VMEM((rounds, own, PAIR * HEAD_DIM), BF16),
            pltpu.VMEM((HALF, own), F32),
            pltpu.VMEM((HALF, own), F32),
            pltpu.VMEM((depth, columns), BF16),
            pltpu.VMEM(scales.shape[:0:-1], F32),
            pltpu.VMEM((PAIR, ROWS, own), F32),
            pltpu.VMEM((rounds, 2, ROWS, HEAD_DIM), F32),
            pltpu.VMEM((rounds, 2, ROWS, HEAD_DIM), F32),
            pltpu.VMEM((rounds, 2, ROWS, HEAD_DIM), F32),
            pltpu.VMEM((rounds, plane, floors, ROWS, HEAD_DIM), BF16),
            pltpu.VMEM((count, GROUPS * HEAD_DIM), BF16),
            pltpu.VMEM((count, columns), F32),
            pltpu.VMEM((count // 2, columns), F32),
            dma((5,)),
            dma((3, pieces)),
            dma((rounds, PAIR)),
            dma,
            dma((rounds,)),
            dma((rounds,)),
            dma,
            dma,
            dma((rounds, max(floors - 1, 1))),
            dma((rounds, max(floors - 1, 1))),
            dma((rounds, max(plane - 1, 1))),
            dma((rounds, max(plane - 1, 1))),
        ],
        compiler_params=pltpu.CompilerParams(
            collective_id=0, has_side_effects=True, vmem_limit_bytes=54 * 1024 * 1024
        ),
        name="decode_step",
    )(lengths, latents[0].T, codes[0], jnp.asarray(cosine), jnp.asarray(sine), scales[0].T,
      queries[0], new_keys[0], new_values[0], key_factor, out_weight)


def solution(mesh):
    placed = (
        P("group"),
        P("group", "kv", None),
        P("group", "kv", None),
        P("group", "kv", None),
        P("group", None, None),
        P("group", None, None),
        P("group", None, None),
        P(),
        P("kv", "group"),
    )
    return jax.shard_map(
        body, mesh=mesh, in_specs=placed, out_specs=P("kv", "group"), check_vma=False
    )
```

```python
import math

import jax
import jax.numpy as jnp
import numpy as np
from jax import lax
from jax.experimental import pallas as pl
from jax.experimental.pallas import tpu as pltpu
from jax.sharding import PartitionSpec as P

HEADS = 64
KV_HEADS = 8
GROUPS = HEADS // KV_HEADS
HEAD_DIM = 128
HALF = HEAD_DIM // 2
BLK = 256
Q_TOK = 8
ROWS = Q_TOK * GROUPS
PAIR = 2
CHUNK = 512
ROPE_BASE = 500000.0
NEG_FILL = -1e30
TO_EXP2 = math.log2(math.e) / math.sqrt(HEAD_DIM)
MESH = pl.DeviceIdType.MESH
F32 = jnp.float32
BF16 = jnp.bfloat16


def rope_tables(ctx):
    exponent = -(np.arange(HALF, dtype=np.float64) * 2.0) / HEAD_DIM
    frequency = (ROPE_BASE**exponent).astype(np.float32)
    angles = frequency[:, None] * np.arange(ctx, dtype=np.float32)[None, :]
    angles = angles.astype(np.float64)
    return np.cos(angles).astype(np.float32), np.sin(angles).astype(np.float32)


def stacked_rows(block):
    wide = block.astype(F32)
    return jnp.concatenate(
        [wide[:, g * HEAD_DIM : (g + 1) * HEAD_DIM] for g in range(GROUPS)], axis=0
    ).astype(BF16)


def padded(block):
    wide = block.astype(F32)
    blank = jnp.zeros((HEAD_DIM - Q_TOK, HEAD_DIM), F32)
    return jnp.concatenate([wide, blank], axis=0).astype(BF16)


def step_kernel(
    length, latents_hbm, codes_hbm, cosine_hbm, sine_hbm, scales_hbm, queries_hbm,
    new_keys_hbm, new_values_hbm, factor_hbm, weight_hbm, out,
    scales_in, queries, late_keys, late_values, factor,
    latents, codes, cosine, sine, weight, scales, scores, state, mine, theirs, got, buffer, rows, partial,
    got_partial,
    small_sem, piece_sem, codes_sem, weight_sem, pair_send, pair_recv, last_send, last_recv,
    column_send, column_recv, plane_send, plane_recv,
):
    at = lax.axis_index("kv")
    other = 1 - at
    me = lax.axis_index("group")
    own = latents.shape[1]
    base = at * own
    rounds = buffer.shape[0]
    plane, floors = buffer.shape[1:3]
    members = plane * floors
    floor, place = me // plane, me % plane
    above = [((floor + d) % floors) * plane + place for d in range(1, floors)]
    beside = [floor * plane + (place + d) % plane for d in range(1, plane)]
    pieces = piece_sem.shape[1]
    wide = own // pieces

    def piece_copies(n):
        span = pl.ds(n * wide, wide)
        there = pl.ds(pl.multiple_of(base + n * wide, wide), wide)
        return [
            pltpu.make_async_copy(latents_hbm.at[:, span], latents.at[:, span], piece_sem.at[0, n]),
            pltpu.make_async_copy(cosine_hbm.at[:, there], cosine.at[:, span], piece_sem.at[1, n]),
            pltpu.make_async_copy(sine_hbm.at[:, there], sine.at[:, span], piece_sem.at[2, n]),
        ]

    def head_of(r, i):
        return (at if i == 0 else other) * rounds + r

    def codes_copies(r):
        result = []
        for i in range(PAIR):
            lanes = pl.ds(pl.multiple_of(head_of(r, i) * HEAD_DIM, HEAD_DIM), HEAD_DIM)
            result.append(
                pltpu.make_async_copy(
                    codes_hbm.at[:, lanes],
                    codes.at[r, :, pl.ds(i * HEAD_DIM, HEAD_DIM)],
                    codes_sem.at[r, i],
                )
            )
        return result

    load = pltpu.make_async_copy(weight_hbm, weight, weight_sem)
    small = [
        pltpu.make_async_copy(source, target, small_sem.at[n])
        for n, (source, target) in enumerate((
            (factor_hbm, factor),
            (queries_hbm, queries),
            (new_keys_hbm, late_keys),
            (new_values_hbm, late_values),
            (scales_hbm, scales_in),
        ))
    ]
    for copy in small:
        copy.start()
    for n in range(pieces):
        for copy in piece_copies(n):
            copy.start()
    for copy in codes_copies(0):
        copy.start()

    barrier = pltpu.get_barrier_semaphore()
    pl.semaphore_signal(barrier, inc=1, device_id=(me, other), device_id_type=MESH)
    for peer in above + beside:
        pl.semaphore_signal(barrier, inc=1, device_id=(peer, at), device_id_type=MESH)
    pl.semaphore_wait(barrier, len(above) + len(beside) + 1)
    for copy in small:
        copy.wait()
    scales[...] = scales_in[...].astype(F32)

    def pair_copy(r):
        return pltpu.make_async_remote_copy(
            src_ref=theirs.at[r], dst_ref=got.at[r], send_sem=pair_send.at[r],
            recv_sem=pair_recv.at[r], device_id=(me, other), device_id_type=MESH,
        )

    def column_copies(r):
        block = buffer.at[r, place, floor]
        return [
            pltpu.make_async_remote_copy(
                src_ref=block, dst_ref=block, send_sem=column_send.at[r, d],
                recv_sem=column_recv.at[r, d], device_id=(peer, at), device_id_type=MESH,
            )
            for d, peer in enumerate(above)
        ]

    def plane_copies(r):
        block = buffer.at[r, place]
        return [
            pltpu.make_async_remote_copy(
                src_ref=block, dst_ref=block, send_sem=plane_send.at[r, d],
                recv_sem=plane_recv.at[r, d], device_id=(peer, at), device_id_type=MESH,
            )
            for d, peer in enumerate(beside)
        ]

    def combine(r):
        pair_copy(r).wait()
        mine_stat, their_stat = mine[r, 1], got[r, 1]
        mine_peak, mine_total = mine_stat[:, :1], mine_stat[:, HALF : HALF + 1]
        their_peak, their_total = their_stat[:, :1], their_stat[:, HALF : HALF + 1]
        peak = jnp.maximum(mine_peak, their_peak)
        mine_scale, their_scale = jnp.exp2(mine_peak - peak), jnp.exp2(their_peak - peak)
        total = mine_total * mine_scale + their_total * their_scale
        joined = (mine[r, 0] * mine_scale + got[r, 0] * their_scale) / total
        buffer[r, place, floor] = joined.astype(BF16)
        for copy in column_copies(r):
            copy.start()

    def spread(r):
        for copy in column_copies(r):
            copy.wait()
        for copy in plane_copies(r):
            copy.start()

    def collect(r):
        for copy in plane_copies(r):
            copy.wait()
        for z in range(floors):
            block = buffer[r, :, z].astype(F32)
            for g in range(GROUPS):
                piece = block[:, g * Q_TOK : (g + 1) * Q_TOK, :].reshape(plane * Q_TOK, HEAD_DIM)
                rows[
                    z * plane * Q_TOK : (z + 1) * plane * Q_TOK,
                    g * HEAD_DIM : (g + 1) * HEAD_DIM,
                ] = piece.astype(BF16)

    depth = GROUPS * HEAD_DIM

    def multiply(r, span):
        layer = weight[pl.ds(pl.multiple_of(r * depth, depth), depth), :]
        partial[span, :] += jnp.dot(rows[span, :], layer, preferred_element_type=F32)

    def whole_product(r):
        collect(r)

        @pl.when(r == 0)
        def _():
            load.wait()

        multiply(r, slice(None))

    column = lax.broadcasted_iota(jnp.int32, (ROWS, HEAD_DIM), 1)
    token = lax.broadcasted_iota(jnp.int32, (ROWS, HEAD_DIM), 0) % Q_TOK
    causal = jnp.logical_and(column <= token, at == 0)
    limit = length[0] - base

    def lanes_of(r, i):
        return pl.ds(pl.multiple_of(head_of(r, i) * HEAD_DIM, HEAD_DIM), HEAD_DIM)

    def prepare(r):
        turned = jnp.concatenate(
            [factor[:, lanes_of(r, i)].astype(F32).T for i in range(PAIR)], axis=0
        ).astype(BF16)
        query = [
            stacked_rows(queries[:, pl.ds(pl.multiple_of(head_of(r, i) * depth, depth), depth)])
            for i in range(PAIR)
        ]
        tops = [jnp.full((ROWS, HEAD_DIM), NEG_FILL, F32) for _ in range(PAIR)]
        return turned, query, tops

    def score_chunk(slot, c, turned, query, tops):
        span = slice(c * CHUNK, (c + 1) * CHUNK)
        keys = jnp.dot(turned, latents[:, span], preferred_element_type=F32)
        cos, sin = cosine[:, span], sine[:, span]
        valid = c * CHUNK + lax.broadcasted_iota(jnp.int32, (1, CHUNK), 1) < limit
        for i in range(PAIR):
            low = keys[i * HEAD_DIM : i * HEAD_DIM + HALF]
            high = keys[i * HEAD_DIM + HALF : (i + 1) * HEAD_DIM]
            rotated = jnp.concatenate(
                [low * cos - high * sin, high * cos + low * sin], axis=0
            ).astype(BF16)
            score = jnp.dot(query[i], rotated, preferred_element_type=F32)
            score = jnp.where(valid, score, NEG_FILL)
            scores[slot, i, :, span] = score
            for v in range(CHUNK // HEAD_DIM):
                tops[i] = jnp.maximum(tops[i], score[:, v * HEAD_DIM : (v + 1) * HEAD_DIM])

    def close_scores(r, query, tops):
        for i in range(PAIR):
            fresh = lax.dot_general(
                query[i], padded(late_keys[:, lanes_of(r, i)]), (((1,), (1,)), ((), ())),
                preferred_element_type=F32,
            )
            fresh = jnp.where(causal, fresh, NEG_FILL)
            peak = jnp.max(jnp.maximum(tops[i], fresh), axis=1, keepdims=True) * TO_EXP2
            weights = jnp.where(causal, jnp.exp2(fresh * TO_EXP2 - peak), 0.0)
            state[0, i] = jnp.broadcast_to(peak, (ROWS, HEAD_DIM))
            state[1, i] = weights
            state[2, i] = jnp.dot(
                weights.astype(BF16), padded(late_values[:, lanes_of(r, i)]),
                preferred_element_type=F32,
            )

    def open_values(r):
        factors = [scales[pl.ds(head_of(r, i), 1), :] for i in range(PAIR)]
        peaks = [state[0, i] for i in range(PAIR)]
        return factors, peaks, [state[1, i] for i in range(PAIR)], [state[2, i] for i in range(PAIR)]

    def value_block(r, slot, b, factors, peaks, totals, parts):
        span = slice(b * BLK, (b + 1) * BLK)
        both = []
        for i in range(PAIR):
            peak = jnp.concatenate([peaks[i]] * (BLK // HEAD_DIM), axis=1)
            weights = jnp.exp2(scores[slot, i, :, span] * TO_EXP2 - peak)
            for v in range(BLK // HEAD_DIM):
                totals[i] = totals[i] + weights[:, v * HEAD_DIM : (v + 1) * HEAD_DIM]
            both.append(weights.astype(BF16))
        product = jnp.dot(
            jnp.concatenate(both, axis=0), codes[r, span, :], preferred_element_type=F32
        )
        for i in range(PAIR):
            own_part = product[i * ROWS : (i + 1) * ROWS, i * HEAD_DIM : (i + 1) * HEAD_DIM]
            parts[i] = parts[i] + own_part * factors[i][:, b : b + 1]

    def close_values(r, factors, peaks, totals, parts):
        for i, keep in ((1, theirs), (0, mine)):
            total = jnp.sum(totals[i], axis=1, keepdims=True)
            keep[r, 0] = parts[i]
            keep[r, 1] = jnp.where(column < HALF, peaks[i], total)
        pair_copy(r).start()

    chunks = own // CHUNK
    blocks = CHUNK // BLK

    def one_round(r, _):
        def hook(action, back):
            @pl.when(r >= back)
            def _():
                action(r - back)

        slot, before = r % 2, (r + 1) % 2
        for copy in codes_copies(r):
            copy.start()
        for copy in codes_copies(r - 1):
            copy.wait()
        ready = prepare(r)
        held = open_values(r - 1)
        for c in range(chunks):
            score_chunk(slot, c, *ready)
            for b in range(c * blocks, (c + 1) * blocks):
                value_block(r - 1, before, b, *held)
            if c == 3:
                hook(combine, 2)
            if c == 5:
                hook(whole_product, 3)
        close_values(r - 1, *held)
        close_scores(r, ready[1], ready[2])
        hook(spread, 2)
        return 0

    partial[...] = jnp.zeros_like(partial)
    ready = prepare(0)
    for c in range(chunks):
        if c * CHUNK % wide == 0:
            for copy in piece_copies(c * CHUNK // wide):
                copy.wait()
        score_chunk(0, c, *ready)
    close_scores(0, ready[1], ready[2])
    load.start()
    lax.fori_loop(1, rounds, one_round, 0)
    last_round = rounds - 1
    for copy in codes_copies(last_round):
        copy.wait()
    held = open_values(last_round)
    for b in range(chunks * blocks):
        value_block(last_round, last_round % 2, b, *held)
        if b == chunks * blocks * 3 // 4 - 1:
            combine(last_round - 1)
    close_values(last_round, *held)
    final = rounds - 1
    combine(final)
    spread(final - 1)
    whole_product(final - 2)
    spread(final)
    whole_product(final - 1)
    collect(final)
    half_rows = members * Q_TOK // 2
    half_of = lambda n: pl.ds(pl.multiple_of(n * half_rows, half_rows), half_rows)
    multiply(final, half_of(other))
    last = pltpu.make_async_remote_copy(
        src_ref=partial.at[half_of(other)], dst_ref=got_partial, send_sem=last_send,
        recv_sem=last_recv, device_id=(me, other), device_id_type=MESH,
    )
    last.start()
    multiply(final, half_of(at))
    last.wait()
    out[...] = partial[half_of(at)] + got_partial[...]


def body(lengths, latents, codes, scales, queries, new_keys, new_values, key_factor, out_weight):
    own, rank = latents.shape[1:]
    cosine, sine = rope_tables(own * lax.axis_size("kv"))
    members = lax.axis_size("group")
    floors = 4 if members % 4 == 0 else 1
    plane = members // floors
    depth, columns = out_weight.shape
    rounds = KV_HEADS // 2
    count = members * Q_TOK
    pieces = 4
    anywhere = pl.BlockSpec(memory_space=pl.ANY)
    scalar = pl.BlockSpec(memory_space=pltpu.SMEM)
    near = pl.BlockSpec(memory_space=pltpu.VMEM)
    dma = pltpu.SemaphoreType.DMA
    return pl.pallas_call(
        step_kernel,
        out_shape=jax.ShapeDtypeStruct((count // 2, columns), F32),
        in_specs=[scalar] + [anywhere] * 10,
        out_specs=near,
        scratch_shapes=[
            pltpu.VMEM(scales.shape[:0:-1], BF16),
            pltpu.VMEM(queries.shape[1:], BF16),
            pltpu.VMEM(new_keys.shape[1:], BF16),
            pltpu.VMEM(new_values.shape[1:], BF16),
            pltpu.VMEM(key_factor.shape, BF16),
            pltpu.VMEM((rank, own), BF16),
            pltpu.VMEM((rounds, own, PAIR * HEAD_DIM), BF16),
            pltpu.VMEM((HALF, own), F32),
            pltpu.VMEM((HALF, own), F32),
            pltpu.VMEM((depth, columns), BF16),
            pltpu.VMEM(scales.shape[:0:-1], F32),
            pltpu.VMEM((2, PAIR, ROWS, own), F32),
            pltpu.VMEM((3, PAIR, ROWS, HEAD_DIM), F32),
            pltpu.VMEM((rounds, 2, ROWS, HEAD_DIM), F32),
            pltpu.VMEM((rounds, 2, ROWS, HEAD_DIM), F32),
            pltpu.VMEM((rounds, 2, ROWS, HEAD_DIM), F32),
            pltpu.VMEM((rounds, plane, floors, ROWS, HEAD_DIM), BF16),
            pltpu.VMEM((count, GROUPS * HEAD_DIM), BF16),
            pltpu.VMEM((count, columns), F32),
            pltpu.VMEM((count // 2, columns), F32),
            dma((5,)),
            dma((3, pieces)),
            dma((rounds, PAIR)),
            dma,
            dma((rounds,)),
            dma((rounds,)),
            dma,
            dma,
            dma((rounds, max(floors - 1, 1))),
            dma((rounds, max(floors - 1, 1))),
            dma((rounds, max(plane - 1, 1))),
            dma((rounds, max(plane - 1, 1))),
        ],
        compiler_params=pltpu.CompilerParams(
            collective_id=0, has_side_effects=True, vmem_limit_bytes=54 * 1024 * 1024
        ),
        name="decode_step",
    )(lengths, latents[0].T, codes[0], jnp.asarray(cosine), jnp.asarray(sine), scales[0].T,
      queries[0], new_keys[0], new_values[0], key_factor, out_weight)


def solution(mesh):
    placed = (
        P("group"),
        P("group", "kv", None),
        P("group", "kv", None),
        P("group", "kv", None),
        P("group", None, None),
        P("group", None, None),
        P("group", None, None),
        P(),
        P("kv", "group"),
    )
    return jax.shard_map(
        body, mesh=mesh, in_specs=placed, out_specs=P("kv", "group"), check_vma=False
    )
```

```python
import math

import jax
import jax.numpy as jnp
import numpy as np
from jax import lax
from jax.experimental import pallas as pl
from jax.experimental.pallas import tpu as pltpu
from jax.sharding import PartitionSpec as P

HEADS = 64
KV_HEADS = 8
GROUPS = HEADS // KV_HEADS
HEAD_DIM = 128
HALF = HEAD_DIM // 2
BLK = 256
Q_TOK = 8
ROWS = Q_TOK * GROUPS
PAIR = 2
CHUNK = 256
ROPE_BASE = 500000.0
NEG_FILL = -1e30
TO_EXP2 = math.log2(math.e) / math.sqrt(HEAD_DIM)
MESH = pl.DeviceIdType.MESH
F32 = jnp.float32
BF16 = jnp.bfloat16


def rope_tables(ctx):
    exponent = -(np.arange(HALF, dtype=np.float64) * 2.0) / HEAD_DIM
    frequency = (ROPE_BASE**exponent).astype(np.float32)
    angles = frequency[:, None] * np.arange(ctx, dtype=np.float32)[None, :]
    angles = angles.astype(np.float64)
    return np.cos(angles).astype(np.float32), np.sin(angles).astype(np.float32)


def stacked_rows(block):
    wide = block.astype(F32)
    return jnp.concatenate(
        [wide[:, g * HEAD_DIM : (g + 1) * HEAD_DIM] for g in range(GROUPS)], axis=0
    ).astype(BF16)


def padded(block):
    wide = block.astype(F32)
    blank = jnp.zeros((HEAD_DIM - Q_TOK, HEAD_DIM), F32)
    return jnp.concatenate([wide, blank], axis=0).astype(BF16)


def step_kernel(
    length, latents_hbm, codes_hbm, cosine_hbm, sine_hbm, scales_hbm, queries_hbm,
    new_keys_hbm, new_values_hbm, factor_hbm, weight_hbm, out,
    scales_in, queries, late_keys, late_values, factor,
    latents, codes, cosine, sine, weight, scales, scores, mine, theirs, got, buffer, rows, partial,
    got_partial,
    small_sem, piece_sem, codes_sem, weight_sem, pair_send, pair_recv, last_send, last_recv,
    column_send, column_recv, plane_send, plane_recv,
):
    at = lax.axis_index("kv")
    other = 1 - at
    me = lax.axis_index("group")
    own = latents.shape[1]
    base = at * own
    rounds = buffer.shape[0]
    plane, floors = buffer.shape[1:3]
    members = plane * floors
    floor, place = me // plane, me % plane
    above = [((floor + d) % floors) * plane + place for d in range(1, floors)]
    beside = [floor * plane + (place + d) % plane for d in range(1, plane)]
    pieces = piece_sem.shape[1]
    wide = own // pieces

    def piece_copies(n):
        span = pl.ds(n * wide, wide)
        there = pl.ds(pl.multiple_of(base + n * wide, wide), wide)
        return [
            pltpu.make_async_copy(latents_hbm.at[:, span], latents.at[:, span], piece_sem.at[0, n]),
            pltpu.make_async_copy(cosine_hbm.at[:, there], cosine.at[:, span], piece_sem.at[1, n]),
            pltpu.make_async_copy(sine_hbm.at[:, there], sine.at[:, span], piece_sem.at[2, n]),
        ]

    def head_of(r, i):
        return (at if i == 0 else other) * rounds + r

    def codes_copies(r):
        result = []
        for i in range(PAIR):
            lanes = pl.ds(pl.multiple_of(head_of(r, i) * HEAD_DIM, HEAD_DIM), HEAD_DIM)
            result.append(
                pltpu.make_async_copy(
                    codes_hbm.at[:, lanes],
                    codes.at[r, :, pl.ds(i * HEAD_DIM, HEAD_DIM)],
                    codes_sem.at[r, i],
                )
            )
        return result

    load = pltpu.make_async_copy(weight_hbm, weight, weight_sem)
    small = [
        pltpu.make_async_copy(source, target, small_sem.at[n])
        for n, (source, target) in enumerate((
            (factor_hbm, factor),
            (queries_hbm, queries),
            (new_keys_hbm, late_keys),
            (new_values_hbm, late_values),
            (scales_hbm, scales_in),
        ))
    ]
    for copy in small:
        copy.start()
    for n in range(pieces):
        for copy in piece_copies(n):
            copy.start()
    for copy in codes_copies(0):
        copy.start()

    barrier = pltpu.get_barrier_semaphore()
    pl.semaphore_signal(barrier, inc=1, device_id=(me, other), device_id_type=MESH)
    for peer in above + beside:
        pl.semaphore_signal(barrier, inc=1, device_id=(peer, at), device_id_type=MESH)
    pl.semaphore_wait(barrier, len(above) + len(beside) + 1)
    for copy in small:
        copy.wait()
    scales[...] = scales_in[...].astype(F32)

    def pair_copy(r):
        return pltpu.make_async_remote_copy(
            src_ref=theirs.at[r], dst_ref=got.at[r], send_sem=pair_send.at[r],
            recv_sem=pair_recv.at[r], device_id=(me, other), device_id_type=MESH,
        )

    def column_copies(r):
        block = buffer.at[r, place, floor]
        return [
            pltpu.make_async_remote_copy(
                src_ref=block, dst_ref=block, send_sem=column_send.at[r, d],
                recv_sem=column_recv.at[r, d], device_id=(peer, at), device_id_type=MESH,
            )
            for d, peer in enumerate(above)
        ]

    def plane_copies(r):
        block = buffer.at[r, place]
        return [
            pltpu.make_async_remote_copy(
                src_ref=block, dst_ref=block, send_sem=plane_send.at[r, d],
                recv_sem=plane_recv.at[r, d], device_id=(peer, at), device_id_type=MESH,
            )
            for d, peer in enumerate(beside)
        ]

    def combine(r):
        pair_copy(r).wait()
        mine_stat, their_stat = mine[r, 1], got[r, 1]
        mine_peak, mine_total = mine_stat[:, :1], mine_stat[:, HALF : HALF + 1]
        their_peak, their_total = their_stat[:, :1], their_stat[:, HALF : HALF + 1]
        peak = jnp.maximum(mine_peak, their_peak)
        mine_scale, their_scale = jnp.exp2(mine_peak - peak), jnp.exp2(their_peak - peak)
        total = mine_total * mine_scale + their_total * their_scale
        joined = (mine[r, 0] * mine_scale + got[r, 0] * their_scale) / total
        buffer[r, place, floor] = joined.astype(BF16)
        for copy in column_copies(r):
            copy.start()

    def spread(r):
        for copy in column_copies(r):
            copy.wait()
        for copy in plane_copies(r):
            copy.start()

    def collect(r):
        for copy in plane_copies(r):
            copy.wait()
        for z in range(floors):
            block = buffer[r, :, z].astype(F32)
            for g in range(GROUPS):
                piece = block[:, g * Q_TOK : (g + 1) * Q_TOK, :].reshape(plane * Q_TOK, HEAD_DIM)
                rows[
                    z * plane * Q_TOK : (z + 1) * plane * Q_TOK,
                    g * HEAD_DIM : (g + 1) * HEAD_DIM,
                ] = piece.astype(BF16)

    depth = GROUPS * HEAD_DIM

    def multiply(r, span):
        layer = weight[pl.ds(pl.multiple_of(r * depth, depth), depth), :]
        partial[span, :] += jnp.dot(rows[span, :], layer, preferred_element_type=F32)

    def whole_product(r):
        collect(r)

        @pl.when(r == 0)
        def _():
            load.wait()

        multiply(r, slice(None))

    column = lax.broadcasted_iota(jnp.int32, (ROWS, HEAD_DIM), 1)
    token = lax.broadcasted_iota(jnp.int32, (ROWS, HEAD_DIM), 0) % Q_TOK
    causal = jnp.logical_and(column <= token, at == 0)
    limit = length[0] - base

    def one_round(r, _):
        def hook(action, back):
            @pl.when(r >= back)
            def _():
                action(r - back)

        lanes = [
            pl.ds(pl.multiple_of(head_of(r, i) * HEAD_DIM, HEAD_DIM), HEAD_DIM)
            for i in range(PAIR)
        ]
        turned = jnp.concatenate(
            [factor[:, lanes[i]].astype(F32).T for i in range(PAIR)], axis=0
        ).astype(BF16)
        query = [
            stacked_rows(queries[:, pl.ds(pl.multiple_of(head_of(r, i) * depth, depth), depth)])
            for i in range(PAIR)
        ]
        factors = [scales[pl.ds(head_of(r, i), 1), :] for i in range(PAIR)]
        tops = [jnp.full((ROWS, HEAD_DIM), NEG_FILL, F32) for _ in range(PAIR)]
        for c in range(own // CHUNK):
            span = slice(c * CHUNK, (c + 1) * CHUNK)
            if c * CHUNK % wide == 0:

                @pl.when(r == 0)
                def _(n=c * CHUNK // wide):
                    for copy in piece_copies(n):
                        copy.wait()

            keys = jnp.dot(turned, latents[:, span], preferred_element_type=F32)
            cos, sin = cosine[:, span], sine[:, span]
            valid = c * CHUNK + lax.broadcasted_iota(jnp.int32, (1, CHUNK), 1) < limit
            for i in range(PAIR):
                low = keys[i * HEAD_DIM : i * HEAD_DIM + HALF]
                high = keys[i * HEAD_DIM + HALF : (i + 1) * HEAD_DIM]
                rotated = jnp.concatenate(
                    [low * cos - high * sin, high * cos + low * sin], axis=0
                ).astype(BF16)
                score = jnp.dot(query[i], rotated, preferred_element_type=F32)
                score = jnp.where(valid, score, NEG_FILL)
                scores[i, :, span] = score
                for v in range(CHUNK // HEAD_DIM):
                    tops[i] = jnp.maximum(tops[i], score[:, v * HEAD_DIM : (v + 1) * HEAD_DIM])
            if c == 3:
                hook(whole_product, 3)
            if c == 7:
                hook(spread, 2)
        hook(combine, 1)
        @pl.when(r == 0)
        def _():
            load.start()

        @pl.when(r + 1 < rounds)
        def _():
            for copy in codes_copies(r + 1):
                copy.start()

        for copy in codes_copies(r):
            copy.wait()
        peaks, totals, parts = [], [], []
        for i in range(PAIR):
            fresh = lax.dot_general(
                query[i], padded(late_keys[:, lanes[i]]), (((1,), (1,)), ((), ())),
                preferred_element_type=F32,
            )
            fresh = jnp.where(causal, fresh, NEG_FILL)
            peak = jnp.max(jnp.maximum(tops[i], fresh), axis=1, keepdims=True) * TO_EXP2
            peaks.append(jnp.broadcast_to(peak, (ROWS, BLK)))
            weights = jnp.where(causal, jnp.exp2(fresh * TO_EXP2 - peak), 0.0)
            totals.append(weights)
            parts.append(
                jnp.dot(
                    weights.astype(BF16), padded(late_values[:, lanes[i]]),
                    preferred_element_type=F32,
                )
            )
        for b in range(own // BLK):
            span = slice(b * BLK, (b + 1) * BLK)
            both = []
            for i in range(PAIR):
                weights = jnp.exp2(scores[i, :, span] * TO_EXP2 - peaks[i])
                for v in range(BLK // HEAD_DIM):
                    totals[i] = totals[i] + weights[:, v * HEAD_DIM : (v + 1) * HEAD_DIM]
                both.append(weights.astype(BF16))
            product = jnp.dot(
                jnp.concatenate(both, axis=0), codes[r, span, :], preferred_element_type=F32
            )
            for i in range(PAIR):
                own_part = product[
                    i * ROWS : (i + 1) * ROWS, i * HEAD_DIM : (i + 1) * HEAD_DIM
                ]
                parts[i] = parts[i] + own_part * factors[i][:, b : b + 1]
        for i, keep in ((1, theirs), (0, mine)):
            total = jnp.sum(totals[i], axis=1, keepdims=True)
            keep[r, 0] = parts[i]
            keep[r, 1] = jnp.where(column < HALF, peaks[i][:, :HEAD_DIM], total)
            if i == 1:
                pair_copy(r).start()
        return 0

    partial[...] = jnp.zeros_like(partial)
    lax.fori_loop(0, rounds, one_round, 0)
    final = rounds - 1
    combine(final)
    spread(final - 1)
    whole_product(final - 2)
    spread(final)
    whole_product(final - 1)
    collect(final)
    half_rows = members * Q_TOK // 2
    half_of = lambda n: pl.ds(pl.multiple_of(n * half_rows, half_rows), half_rows)
    multiply(final, half_of(other))
    last = pltpu.make_async_remote_copy(
        src_ref=partial.at[half_of(other)], dst_ref=got_partial, send_sem=last_send,
        recv_sem=last_recv, device_id=(me, other), device_id_type=MESH,
    )
    last.start()
    multiply(final, half_of(at))
    last.wait()
    out[...] = partial[half_of(at)] + got_partial[...]


def body(lengths, latents, codes, scales, queries, new_keys, new_values, key_factor, out_weight):
    own, rank = latents.shape[1:]
    cosine, sine = rope_tables(own * lax.axis_size("kv"))
    members = lax.axis_size("group")
    floors = 4 if members % 4 == 0 else 1
    plane = members // floors
    depth, columns = out_weight.shape
    rounds = KV_HEADS // 2
    count = members * Q_TOK
    pieces = 4
    anywhere = pl.BlockSpec(memory_space=pl.ANY)
    scalar = pl.BlockSpec(memory_space=pltpu.SMEM)
    near = pl.BlockSpec(memory_space=pltpu.VMEM)
    dma = pltpu.SemaphoreType.DMA
    return pl.pallas_call(
        step_kernel,
        out_shape=jax.ShapeDtypeStruct((count // 2, columns), F32),
        in_specs=[scalar] + [anywhere] * 10,
        out_specs=near,
        scratch_shapes=[
            pltpu.VMEM(scales.shape[:0:-1], BF16),
            pltpu.VMEM(queries.shape[1:], BF16),
            pltpu.VMEM(new_keys.shape[1:], BF16),
            pltpu.VMEM(new_values.shape[1:], BF16),
            pltpu.VMEM(key_factor.shape, BF16),
            pltpu.VMEM((rank, own), BF16),
            pltpu.VMEM((rounds, own, PAIR * HEAD_DIM), BF16),
            pltpu.VMEM((HALF, own), F32),
            pltpu.VMEM((HALF, own), F32),
            pltpu.VMEM((depth, columns), BF16),
            pltpu.VMEM(scales.shape[:0:-1], F32),
            pltpu.VMEM((PAIR, ROWS, own), F32),
            pltpu.VMEM((rounds, 2, ROWS, HEAD_DIM), F32),
            pltpu.VMEM((rounds, 2, ROWS, HEAD_DIM), F32),
            pltpu.VMEM((rounds, 2, ROWS, HEAD_DIM), F32),
            pltpu.VMEM((rounds, plane, floors, ROWS, HEAD_DIM), BF16),
            pltpu.VMEM((count, GROUPS * HEAD_DIM), BF16),
            pltpu.VMEM((count, columns), F32),
            pltpu.VMEM((count // 2, columns), F32),
            dma((5,)),
            dma((3, pieces)),
            dma((rounds, PAIR)),
            dma,
            dma((rounds,)),
            dma((rounds,)),
            dma,
            dma,
            dma((rounds, max(floors - 1, 1))),
            dma((rounds, max(floors - 1, 1))),
            dma((rounds, max(plane - 1, 1))),
            dma((rounds, max(plane - 1, 1))),
        ],
        compiler_params=pltpu.CompilerParams(
            collective_id=0, has_side_effects=True, vmem_limit_bytes=54 * 1024 * 1024
        ),
        name="decode_step",
    )(lengths, latents[0].T, codes[0], jnp.asarray(cosine), jnp.asarray(sine), scales[0].T,
      queries[0], new_keys[0], new_values[0], key_factor, out_weight)


def solution(mesh):
    placed = (
        P("group"),
        P("group", "kv", None),
        P("group", "kv", None),
        P("group", "kv", None),
        P("group", None, None),
        P("group", None, None),
        P("group", None, None),
        P(),
        P("kv", "group"),
    )
    return jax.shard_map(
        body, mesh=mesh, in_specs=placed, out_specs=P("kv", "group"), check_vma=False
    )
```
